32 devices in a mesh: seq: 8 (over z, x), head: 4 (over y, core).
Axes of the slice: x: 2, y: 2, z: 4, core: 2. Of those that a mesh axis runs over, the one named last changes fastest.
Arguments:
- queries: bfloat16 [8192, 8192], P('seq', 'head'), may hold values from -0.5390625 to 0.5390625
- keys: bfloat16 [8192, 8192], P('seq', 'head'), may hold values from -0.5390625 to 0.5390625
- values: bfloat16 [8192, 8192], P('seq', 'head'), may hold values from -6 to 6
- log_decay: float32 [8192, 64], P('seq', 'head'), may hold values from -1 to 0
- gain: float32 [8192], P('head'), may hold values from 0.1 to 1.9
- lengths: int32 [8], replicated, may hold values from 1 to 2048, 8192 in all
- out_grad: bfloat16 [8192, 8192], P('seq', 'head'), may hold values from -6 to 6
Outputs:
- normed: bfloat16 [8192, 8192], P('seq', 'head')
- grad_query: bfloat16 [8192, 8192], P('seq', 'head')
- grad_key: bfloat16 [8192, 8192], P('seq', 'head')
- grad_value: bfloat16 [8192, 8192], P('seq', 'head')
The draws below stay inside these ranges and needn't reach their ends.
Inputs may be any that keep to these rules, and one draw needn't show every extreme that they name: The 8 lengths sum to 8192.
All inputs are finite; a program needn't handle non-finite values.
Results may differ from the reference program's by a relative error of at most 0.012.
Values sent between devices are 32-bit elements; how exact they have to be, the bound alone decides.
No kernel may reach another device: no remote copies, remote signals or barrier semaphores. Data moves between devices by JAX's collectives and lax.ppermute only.
A program may use at most 192 MiB of HBM per device.

```python
import math
import jax
import jax.numpy as jnp
import numpy as np
from jax import lax

HEAD_COUNT = 64
HD = 128
TOK_DEV = 1024
DOCS = 8
TOKEN_COUNT = 8192


def draw_log_decay(key, part):
    random_subkeys = jax.random.split(jax.random.fold_in(key, 11), 7)
    quick_share = 0.5
    fast_heads = jax.random.uniform(random_subkeys[0], (HEAD_COUNT,)) < quick_share
    slow_rate = jnp.log(10.0) / (3.0 * TOKEN_COUNT) * jax.random.uniform(random_subkeys[1], (HEAD_COUNT,), minval=0.3, maxval=1.0)
    fast_rate = 1.0 / jax.random.uniform(random_subkeys[2], (HEAD_COUNT,), minval=30.0, maxval=50.0)
    decay_rate = jnp.where(fast_heads, fast_rate, slow_rate)
    shards = TOKEN_COUNT // TOK_DEV
    factor = jnp.exp(jax.random.uniform(random_subkeys[3], (shards, 1, HEAD_COUNT), minval=-0.7, maxval=0.7))
    roughness = jax.random.uniform(random_subkeys[4], (shards, TOK_DEV, HEAD_COUNT), minval=0.5, maxval=1.5)
    logarithm_rates = -(decay_rate * factor * roughness).reshape(TOKEN_COUNT, HEAD_COUNT)
    spike_rows = jax.random.randint(random_subkeys[5], (3,), 0, TOKEN_COUNT)
    masked_entries = jnp.any(jnp.arange(TOKEN_COUNT)[:, None] == spike_rows[None, :], axis=1)
    spike_loss = jnp.log(jax.random.uniform(random_subkeys[6], (TOKEN_COUNT, HEAD_COUNT), minval=0.5, maxval=0.8))
    return (logarithm_rates + jnp.where(masked_entries[:, None], spike_loss, 0.0)).astype(jnp.float32)


def steps_of(stream_key, extent, pieces, low, top_value):
    level, own = 1.0, jax.random.fold_in(stream_key, 6)
    for axis_at, shards_of in pieces:
        draws = jnp.exp(jax.random.uniform(jax.random.fold_in(own, axis_at), (shards_of,), jnp.float32, low / len(pieces), top_value / len(pieces)))
        level = level * jnp.repeat(draws, extent[axis_at] // shards_of).reshape([-1 if axis == axis_at else 1 for axis in range(len(extent))])
    return level


def profile(amount, total, reach, slope):
    portions = [(1 << 20) // math.isqrt(grade ** slope) + 1 for grade in range(2, amount + 1)]
    spare, given = total - reach - (amount - 1), [1] * (amount - 1)
    while spare > 0:
        candidates = [i for i in range(amount - 1) if given[i] < reach]
        whole, budget = sum([portions[i] for i in candidates]), spare
        for i in candidates:
            more = min(reach - given[i], max(1, budget * portions[i] // whole), spare)
            given[i] = given[i] + more
            spare = spare - more
    return np.array([reach] + given)


def uneven_parts(stream_key, count, total, most, slope):
    if count == 2:
        one = jax.random.randint(stream_key, (), max(1, total - most), min(most, total - 1) + 1)
        return jnp.stack([one, total - one])
    sizes = jnp.asarray(profile(count, total, most, slope), jnp.int32)
    couples = (count - 1) // 2
    donor, sink = sizes[1:1 + 2 * couples:2], sizes[2:2 + 2 * couples:2]
    slack = jnp.minimum(donor - 1, most - sink)
    moved = jax.random.randint(jax.random.fold_in(stream_key, 1), (couples,), 0, 1 << 20) % (slack + 1)
    sizes = sizes.at[1:1 + 2 * couples:2].set(donor - moved).at[2:2 + 2 * couples:2].set(sink + moved)
    return sizes[jax.random.permutation(jax.random.fold_in(stream_key, 2), count)]


def normal_values(own_key, extent, deviation, limit, cuts=(), kind=jnp.bfloat16):
    entries = deviation * jax.random.normal(own_key, extent, jnp.float32)
    if cuts:
        entries = entries * steps_of(own_key, extent, cuts, -0.22, 0.18)
    return jnp.clip(entries, -limit, limit).astype(kind)


def setup_inputs(seed: int = 0) -> dict:
    splits = jax.random.split(jax.random.key(seed), 8)
    return {
        "queries": normal_values(splits[0], (TOKEN_COUNT, HEAD_COUNT * HD), 0.09, 0.5390625, ((0, 8), (1, 4))),
        "keys": normal_values(splits[1], (TOKEN_COUNT, HEAD_COUNT * HD), 0.09, 0.5390625, ((0, 8), (1, 4))),
        "values": normal_values(splits[2], (TOKEN_COUNT, HEAD_COUNT * HD), 1.0, 6.0, ((0, 8), (1, 4))),
        "log_decay": draw_log_decay(jax.random.fold_in(splits[7], 71), 0),
        "gain": jnp.clip(1.0 + 0.18 * jax.random.normal(splits[4], (HEAD_COUNT * HD,), jnp.float32), 0.1, 1.9),
        "lengths": uneven_parts(splits[5], DOCS, TOKEN_COUNT, TOKEN_COUNT // 4, 2).astype(jnp.int32),
        "out_grad": normal_values(splits[6], (TOKEN_COUNT, HEAD_COUNT * HD), 1.0, 6.0, ((0, 8), (1, 4))),
    }


exact_mode = lax.Precision.HIGHEST
epsilon = 1e-06

def rounded(array):
    return lax.optimization_barrier(array.astype(jnp.bfloat16)).astype(jnp.float32)

def doc_numbers(lengths, first_row, row_count):
    doc_ends = jnp.cumsum(lengths).astype(jnp.int32)
    places = (first_row + jnp.arange(row_count, dtype=jnp.int32)).astype(jnp.int32)
    counted = lax.optimization_barrier(jnp.sum((places[:, None] >= doc_ends[None, :]).astype(jnp.int32), axis=1)).astype(jnp.int32)
    return jnp.where(places >= 0, counted, -1).astype(jnp.int32)

def edge_factors(logarithm_rates, doc_ids, doc_before):
    running = jnp.cumsum(logarithm_rates, axis=0)
    enter_gain = jnp.exp(running) * (doc_ids == doc_before).astype(running.dtype)[:, None]
    leave_gain = jnp.exp(running[-1][None, :] - running) * (doc_ids == doc_ids[-1]).astype(running.dtype)[:, None]
    keep_gain = jnp.exp(running[-1]) * (doc_ids[-1] == doc_before).astype(running.dtype)
    return (running, enter_gain, leave_gain, keep_gain)

def block_factors(logarithm_rates, doc_ids, doc_before):
    running, enter_gain, leave_gain, keep_gain = edge_factors(logarithm_rates, doc_ids, doc_before)
    block_len = doc_ids.shape[0]
    causal = jnp.arange(block_len)[:, None] >= jnp.arange(block_len)[None, :]
    same_doc = (causal & (doc_ids[:, None] == doc_ids[None, :]))[None]
    log_gap = running.T[:, :, None] - running.T[:, None, :]
    weights = jnp.where(same_doc, jnp.exp(jnp.where(same_doc, log_gap, 0.0)), 0.0)
    return (weights, enter_gain, leave_gain, keep_gain)

def reference(queries, keys, values, log_decay, gain, lengths, out_grad):
    full_width = HEAD_COUNT * HD
    block_len = min(128, TOKEN_COUNT)
    blocks = TOKEN_COUNT // block_len

    def by_heads(array):
        return array.reshape(blocks, block_len, HEAD_COUNT, HD)
    doc_ids = doc_numbers(lengths, 0, TOKEN_COUNT).reshape(blocks, block_len)
    starts = jnp.concatenate([jnp.full((1,), -1, jnp.int32), doc_ids[:-1, -1]]).astype(jnp.int32)
    gains = gain.astype(jnp.float32)
    rate_blocks = log_decay.reshape(blocks, block_len, HEAD_COUNT)

    def forward(states, block_item):
        query_blk, key_blk, value_blk, grad_blk, rate_blk, doc_blk, start_doc = block_item
        query_blk = query_blk.astype(jnp.float32)
        key_blk = key_blk.astype(jnp.float32)
        value_blk = value_blk.astype(jnp.float32)
        weights, enter_gain, leave_gain, keep_gain = block_factors(rate_blk, doc_blk, start_doc)
        state_half = rounded(states)
        probs = rounded(jnp.einsum('shd,thd->hst', query_blk, key_blk, precision=exact_mode) * weights)
        raw_out = jnp.einsum('hst,thd->shd', probs, value_blk, precision=exact_mode)
        raw_out = raw_out + enter_gain[:, :, None] * jnp.einsum('shd,hde->she', query_blk, state_half, precision=exact_mode)
        flattened = raw_out.reshape(block_len, full_width)
        inverse = lax.rsqrt(lax.optimization_barrier(jnp.sum(flattened * flattened, axis=1, keepdims=True)) / full_width + epsilon)
        normed = flattened * inverse * gains
        scaled = grad_blk.astype(jnp.float32) * gains
        projected = lax.optimization_barrier(jnp.sum(scaled * flattened, axis=1, keepdims=True))
        grad_flat = inverse * scaled - flattened * inverse ** 3 * projected / full_width
        grad_raw = rounded(grad_flat).reshape(block_len, HEAD_COUNT, HD)
        mixed = rounded(jnp.einsum('shd,thd->hst', grad_raw, value_blk, precision=exact_mode) * weights)
        grad_query = jnp.einsum('hst,thd->shd', mixed, key_blk, precision=exact_mode)
        grad_query = grad_query + enter_gain[:, :, None] * jnp.einsum('hde,she->shd', state_half, grad_raw, precision=exact_mode)
        update = jnp.einsum('thd,the->hde', rounded(key_blk * leave_gain[:, :, None]), value_blk, precision=exact_mode)
        return (keep_gain[:, None, None] * states + update, (normed, grad_raw, grad_query))
    zero_state = jnp.zeros((HEAD_COUNT, HD, HD), jnp.float32)
    inputs = (by_heads(queries), by_heads(keys), by_heads(values), out_grad.reshape(blocks, block_len, full_width), rate_blocks, doc_ids, starts)
    last_state, (normed, grad_raw, grad_query) = lax.scan(forward, zero_state, inputs)

    def backward(carried, block_item):
        query_blk, key_blk, value_blk, rate_blk, doc_blk, start_doc, grad_blk = block_item
        query_blk = query_blk.astype(jnp.float32)
        key_blk = key_blk.astype(jnp.float32)
        value_blk = value_blk.astype(jnp.float32)
        weights, enter_gain, leave_gain, keep_gain = block_factors(rate_blk, doc_blk, start_doc)
        carried_half = rounded(carried)
        probs = rounded(jnp.einsum('shd,thd->hst', query_blk, key_blk, precision=exact_mode) * weights)
        mixed = rounded(jnp.einsum('shd,thd->hst', grad_blk, value_blk, precision=exact_mode) * weights)
        grad_key = jnp.einsum('hst,shd->thd', mixed, query_blk, precision=exact_mode)
        grad_key = grad_key + leave_gain[:, :, None] * jnp.einsum('hde,the->thd', carried_half, value_blk, precision=exact_mode)
        grad_value = jnp.einsum('hst,she->the', probs, grad_blk, precision=exact_mode)
        grad_value = grad_value + leave_gain[:, :, None] * jnp.einsum('hde,thd->the', carried_half, key_blk, precision=exact_mode)
        update = jnp.einsum('shd,she->hde', rounded(query_blk * enter_gain[:, :, None]), grad_blk, precision=exact_mode)
        return (keep_gain[:, None, None] * carried + update, (grad_key, grad_value))
    back_inputs = (by_heads(queries), by_heads(keys), by_heads(values), rate_blocks, doc_ids, starts, grad_raw)
    first_carry, (grad_key, grad_value) = lax.scan(backward, zero_state, back_inputs, reverse=True)
    shape_out = (TOKEN_COUNT, full_width)
    return (normed.reshape(shape_out).astype(jnp.bfloat16), grad_query.reshape(shape_out).astype(jnp.bfloat16), grad_key.reshape(shape_out).astype(jnp.bfloat16), grad_value.reshape(shape_out).astype(jnp.bfloat16))
```

```python
import functools

import jax
import jax.numpy as jnp
from jax import lax
from jax.experimental import pallas as pl
from jax.experimental.pallas import tpu as pltpu
from jax.sharding import PartitionSpec as P

BLOCK = 128
LANES = 128
EPS = 1e-06
F32 = jnp.float32
BF16 = jnp.bfloat16
VMEM_LIMIT = 58 * 1024 * 1024
DOC_SHARE = 4


def dot_nn(left, right):
    return lax.dot_general(left, right, (((1,), (0,)), ((), ())), preferred_element_type=F32)


def dot_nt(left, right):
    return lax.dot_general(left, right, (((1,), (1,)), ((), ())), preferred_element_type=F32)


def dot_tn(left, right):
    return lax.dot_general(left, right, (((0,), (0,)), ((), ())), preferred_element_type=F32)


def head_cols(index, size):
    return slice(index * size, (index + 1) * size)


def scaled_half(array, factor):
    return (array.astype(F32) * factor).astype(BF16)


def spec(shape, index_map):
    return pl.BlockSpec(shape, index_map)


def whole_spec(shape):
    rank = len(shape)
    return pl.BlockSpec(shape, lambda i: (0,) * rank)


def params():
    return pltpu.CompilerParams(vmem_limit_bytes=VMEM_LIMIT)


def cost(flops, bytes_accessed):
    return pl.CostEstimate(flops=flops, bytes_accessed=bytes_accessed, transcendentals=0)


RUN, ENTER, LEAVE, ENTER_DEV, LEAVE_DEV = range(5)


def count_docs(place, ends):
    total = jnp.zeros_like(place)
    for end in ends:
        total = total + (place >= end).astype(jnp.int32)
    return total


def write_factors(heads, docs, rate_ref, len_ref, first_ref, col_ref, row_ref, keep_ref, keep_dev_ref):
    rows = rate_ref.shape[0]
    blocks = rows // BLOCK
    first = first_ref[0]
    ends, total = [], 0
    for i in range(docs):
        total = total + len_ref[i]
        ends.append(total)

    def doc_at(place):
        return jnp.where(place >= 0, count_docs(place, ends), -1)

    tri = (
        lax.broadcasted_iota(jnp.int32, (BLOCK, BLOCK), 0)
        >= lax.broadcasted_iota(jnp.int32, (BLOCK, BLOCK), 1)
    ).astype(F32)
    runs, offsets = [], []
    offset = jnp.zeros((1, heads), F32)
    for b in range(blocks):
        rates = rate_ref[b * BLOCK : (b + 1) * BLOCK, :]
        run = lax.dot_general(
            tri, rates, (((1,), (0,)), ((), ())),
            precision=lax.Precision.HIGHEST, preferred_element_type=F32,
        )
        run_rows = lax.dot_general(
            rates, tri, (((0,), (1,)), ((), ())),
            precision=lax.Precision.HIGHEST, preferred_element_type=F32,
        )
        row_ref[0:heads, b * BLOCK : (b + 1) * BLOCK] = run_rows
        runs.append(run)
        offsets.append(offset)
        offset = offset + run[BLOCK - 1 : BLOCK, :]
    doc_before = doc_at(first - 1)
    doc_end = doc_at(first + rows - 1)
    prefix = jnp.ones((1, heads), F32)
    keep_ref[...] = jnp.zeros_like(keep_ref)
    keep_dev = jnp.exp(offset) * (doc_end == doc_before).astype(F32)
    keep_dev_ref[...] = jnp.zeros_like(keep_dev_ref)
    keep_dev_ref[0:1, 0:heads] = keep_dev
    for b in range(blocks):
        low = b * BLOCK
        rows_at = slice(low, low + BLOCK)
        place = first + low + lax.broadcasted_iota(jnp.int32, (BLOCK, 1), 0)
        doc = count_docs(place, ends)
        doc_start = doc_at(first + low - 1)
        doc_last = doc_at(first + low + BLOCK - 1)
        run = runs[b]
        last = run[BLOCK - 1 : BLOCK, :]
        run_dev = offsets[b] + run
        groups = (
            run,
            jnp.exp(run) * (doc == doc_start).astype(F32),
            jnp.exp(last - run) * (doc == doc_last).astype(F32),
            jnp.exp(run_dev) * (doc == doc_before).astype(F32),
            jnp.exp(offset - run_dev) * (doc == doc_end).astype(F32),
        )
        for g, group in enumerate(groups):
            col_ref[rows_at, g * heads : (g + 1) * heads] = group
        col_ref[rows_at, len(groups) * heads : len(groups) * heads + 1] = doc.astype(F32)
        keep = jnp.exp(last) * (doc_last == doc_start).astype(F32)
        keep_ref[b, 0:1, 0:heads] = keep
        keep_ref[b, 1:2, 0:heads] = prefix
        prefix = prefix * keep
    place = first + lax.broadcasted_iota(jnp.int32, (1, rows), 1)
    row_ref[heads : heads + 1, :] = count_docs(place, ends).astype(F32)


def state_kernel(
    heads, size, docs, len_ref, first_ref, rate_ref, key_ref, value_ref,
    state_ref, col_ref, row_ref, keep_ref, keep_dev_ref,
):
    step = pl.program_id(0)
    rows = key_ref.shape[0]

    @pl.when(step == 0)
    def _():
        write_factors(heads, docs, rate_ref, len_ref, first_ref, col_ref, row_ref, keep_ref, keep_dev_ref)
        state_ref[...] = jnp.zeros_like(state_ref)

    col = col_ref[pl.ds(pl.multiple_of(step * rows, rows), rows), :]
    for h in range(heads):
        leave = col[:, LEAVE_DEV * heads + h : LEAVE_DEV * heads + h + 1]
        weighted = scaled_half(key_ref[:, head_cols(h, size)], leave)
        state_ref[h] += dot_tn(weighted, value_ref[:, head_cols(h, size)])


def local_states(keys, values, rates, lengths, first, heads, size):
    rows, width = keys.shape
    docs = lengths.shape[0]
    step_rows = min(256, rows)
    blocks = rows // BLOCK
    row_count = -(-(heads + 1) // 8) * 8
    shapes = (
        (heads, size, size),
        (rows, LANES),
        (row_count, rows),
        (blocks, 8, LANES),
        (8, LANES),
    )
    smem = pl.BlockSpec(memory_space=pltpu.SMEM)
    return pl.pallas_call(
        functools.partial(state_kernel, heads, size, docs),
        grid=(rows // step_rows,),
        in_specs=[
            smem,
            smem,
            whole_spec((rows, heads)),
            spec((step_rows, width), lambda i: (i, 0)),
            spec((step_rows, width), lambda i: (i, 0)),
        ],
        out_specs=[whole_spec(s) for s in shapes],
        out_shape=[jax.ShapeDtypeStruct(s, F32) for s in shapes],
        compiler_params=params(),
        cost_estimate=cost(2 * rows * width * size, 4 * rows * width),
        name="local_state",
    )(lengths, first, rates, keys, values)


def block_weights(heads, col, rows_ref, h, bias):
    return jnp.exp(col[:, RUN * heads + h : RUN * heads + h + 1] - rows_ref[h : h + 1, :] + bias)


def block_bias(heads, col, rows_ref):
    doc_col = col[:, 5 * heads : 5 * heads + 1]
    doc_row = rows_ref[heads : heads + 1, :]
    causal = lax.broadcasted_iota(jnp.int32, (BLOCK, BLOCK), 0) >= lax.broadcasted_iota(
        jnp.int32, (BLOCK, BLOCK), 1
    )
    return jnp.where(causal & (doc_col == doc_row), 0.0, -1e30)


def forward_kernel(
    heads, size, query_ref, key_ref, value_ref, col_ref, row_ref, keep_ref,
    raw_ref, probs_ref, states_ref, state_ref,
):
    step = pl.program_id(0)

    @pl.when(step == 0)
    def _():
        state_ref[...] = jnp.zeros_like(state_ref)

    col = col_ref[...]
    bias = block_bias(heads, col, row_ref)
    for h in range(heads):
        at = head_cols(h, size)
        query, key, value = query_ref[:, at], key_ref[:, at], value_ref[:, at]
        enter = col[:, ENTER * heads + h : ENTER * heads + h + 1]
        leave = col[:, LEAVE * heads + h : LEAVE * heads + h + 1]
        weights = block_weights(heads, col, row_ref, h, bias)
        probs = (dot_nt(query, key) * weights).astype(BF16)
        state = state_ref[h]
        state_half = state.astype(BF16)
        probs_ref[0, h] = probs
        states_ref[0, h] = state_half
        both = jnp.concatenate([probs, scaled_half(query, enter)], axis=1)
        raw = dot_nn(both, jnp.concatenate([value, state_half], axis=0))
        raw_ref[:, at] = raw.astype(BF16)
        state_ref[h] = keep_ref[0, 0:1, h : h + 1] * state + dot_tn(scaled_half(key, leave), value)


def forward_local(queries, keys, values, col, row, keep, heads, size):
    rows, width = queries.shape
    blocks = rows // BLOCK
    token = spec((BLOCK, width), lambda i: (i, 0))
    per_block = spec((1, heads, size, size), lambda i: (i, 0, 0, 0))
    return pl.pallas_call(
        functools.partial(forward_kernel, heads, size),
        grid=(blocks,),
        in_specs=[
            token,
            token,
            token,
            spec((BLOCK, LANES), lambda i: (i, 0)),
            spec((row.shape[0], BLOCK), lambda i: (0, i)),
            spec((1, 8, LANES), lambda i: (i, 0, 0)),
        ],
        out_specs=[token, per_block, per_block],
        out_shape=[
            jax.ShapeDtypeStruct((rows, width), BF16),
            jax.ShapeDtypeStruct((blocks, heads, BLOCK, BLOCK), BF16),
            jax.ShapeDtypeStruct((blocks, heads, size, size), BF16),
        ],
        scratch_shapes=[pltpu.VMEM((heads, size, size), F32)],
        compiler_params=params(),
        cost_estimate=cost(8 * rows * width * size, 12 * rows * width),
        name="forward_local",
    )(queries, keys, values, col, row, keep)


def horner(received, keeps, h):
    total = received[-1][h]
    for state, keep in zip(reversed(received[:-1]), reversed(keeps)):
        total = state[h] + keep[0:1, h : h + 1] * total
    return total


def raw_kernel(heads, size, hops, raw_ref, query_ref, grad_ref, gain_ref, col_ref, *rest):
    received, keeps = rest[:hops], rest[hops : 2 * hops - 1]
    out_ref, sums_ref, enter_ref = rest[2 * hops - 1 :]
    step = pl.program_id(0)
    rows = raw_ref.shape[0]

    @pl.when(step == 0)
    def _():
        for h in range(heads):
            enter_ref[h] = horner(received, keeps, h).astype(BF16)

    col = col_ref[...]
    squares = jnp.zeros((rows, size), F32)
    projected = jnp.zeros((rows, size), F32)
    for h in range(heads):
        at = head_cols(h, size)
        enter = col[:, ENTER_DEV * heads + h : ENTER_DEV * heads + h + 1]
        raw = raw_ref[:, at].astype(F32) + enter * dot_nn(query_ref[:, at], enter_ref[h])
        out_ref[:, at] = raw.astype(BF16)
        squares = squares + raw * raw
        projected = projected + grad_ref[:, at].astype(F32) * gain_ref[:, at] * raw
    lane = lax.broadcasted_iota(jnp.int32, (rows, LANES), 1)
    packed = jnp.where(
        lane == 0,
        jnp.sum(squares, axis=1, keepdims=True),
        jnp.where(lane == 1, jnp.sum(projected, axis=1, keepdims=True), 0.0),
    )
    sums_ref[...] = packed.T[0:8, :]


def raw_and_sums(raw, queries, out_grad, gain, col, received, keeps, heads, size):
    rows, width = queries.shape
    step_rows = min(256, rows)
    token = spec((step_rows, width), lambda i: (i, 0))
    state_shape = (heads, size, size)
    return pl.pallas_call(
        functools.partial(raw_kernel, heads, size, len(received)),
        grid=(rows // step_rows,),
        in_specs=[
            token,
            token,
            token,
            whole_spec((1, width)),
            spec((step_rows, LANES), lambda i: (i, 0)),
        ]
        + [whole_spec(state_shape)] * len(received)
        + [whole_spec((8, LANES))] * len(keeps),
        out_specs=[token, spec((8, step_rows), lambda i: (0, i)), whole_spec(state_shape)],
        out_shape=[
            jax.ShapeDtypeStruct((rows, width), BF16),
            jax.ShapeDtypeStruct((8, rows), F32),
            jax.ShapeDtypeStruct(state_shape, BF16),
        ],
        compiler_params=params(),
        cost_estimate=cost(2 * rows * width * size, 8 * rows * width),
        name="raw_and_sums",
    )(raw, queries, out_grad, gain, col, *received, *keeps)


def carry_kernel(heads, size, full_width, parts, raw_ref, query_ref, grad_ref, gain_ref, col_ref, *rest):
    sums = rest[:parts]
    carry_ref, scale_ref = rest[parts:]
    step = pl.program_id(0)
    rows = raw_ref.shape[0]

    @pl.when(step == 0)
    def _():
        carry_ref[...] = jnp.zeros_like(carry_ref)

    total = sums[0][...]
    for part in sums[1:]:
        total = total + part[...]
    total = jnp.concatenate([total, jnp.zeros((LANES - 8, rows), F32)], axis=0).T
    inverse = lax.rsqrt(total[:, 0:1] / full_width + EPS)
    slope = inverse * inverse * inverse * total[:, 1:2] / full_width
    lane = lax.broadcasted_iota(jnp.int32, (rows, LANES), 1)
    scale_ref[...] = jnp.where(lane == 0, inverse, slope)
    col = col_ref[...]
    for h in range(heads):
        at = head_cols(h, size)
        enter = col[:, ENTER_DEV * heads + h : ENTER_DEV * heads + h + 1]
        scaled = grad_ref[:, at].astype(F32) * gain_ref[:, at]
        grad_raw = (inverse * scaled - raw_ref[:, at].astype(F32) * slope).astype(BF16)
        carry_ref[h] += dot_tn(scaled_half(query_ref[:, at], enter), grad_raw)


def carry_states(raw, queries, out_grad, gain, col, sums, full_width, heads, size):
    rows, width = queries.shape
    step_rows = min(256, rows)
    token = spec((step_rows, width), lambda i: (i, 0))
    narrow = spec((step_rows, LANES), lambda i: (i, 0))
    state_shape = (heads, size, size)
    return pl.pallas_call(
        functools.partial(carry_kernel, heads, size, full_width, len(sums)),
        grid=(rows // step_rows,),
        in_specs=[token, token, token, whole_spec((1, width)), narrow]
        + [spec((8, step_rows), lambda i: (0, i))] * len(sums),
        out_specs=[whole_spec(state_shape), narrow],
        out_shape=[
            jax.ShapeDtypeStruct(state_shape, F32),
            jax.ShapeDtypeStruct((rows, LANES), F32),
        ],
        compiler_params=params(),
        cost_estimate=cost(2 * rows * width * size, 6 * rows * width),
        name="carry_state",
    )(raw, queries, out_grad, gain, col, *sums)


def backward_kernel(
    heads, size, query_ref, key_ref, value_ref, raw_ref, out_grad_ref, gain_ref, scale_ref,
    col_ref, row_ref, keep_ref, probs_ref, states_ref, enter_ref,
    normed_ref, grad_query_ref, grad_key_ref, grad_value_ref, carry_ref,
):
    step = pl.program_id(0)

    @pl.when(step == 0)
    def _():
        carry_ref[...] = jnp.zeros_like(carry_ref)

    col = col_ref[...]
    bias = block_bias(heads, col, row_ref)
    inverse, slope = scale_ref[:, 0:1], scale_ref[:, 1:2]
    for h in range(heads):
        at = head_cols(h, size)
        query, key, value = query_ref[:, at], key_ref[:, at], value_ref[:, at]
        raw, gain = raw_ref[:, at].astype(F32), gain_ref[:, at]
        enter = col[:, ENTER * heads + h : ENTER * heads + h + 1]
        leave = col[:, LEAVE * heads + h : LEAVE * heads + h + 1]
        grad_raw = (inverse * (out_grad_ref[:, at].astype(F32) * gain) - raw * slope).astype(BF16)
        normed_ref[:, at] = (raw * inverse * gain).astype(BF16)
        weights = block_weights(heads, col, row_ref, h, bias)
        mixed = (dot_nt(grad_raw, value) * weights).astype(BF16)
        prefix = keep_ref[0, 1:2, h : h + 1]
        state = (states_ref[0, h].astype(F32) + prefix * enter_ref[h].astype(F32)).astype(BF16)
        grad_query = dot_nn(mixed, key) + enter * dot_nt(grad_raw, state)
        grad_query_ref[:, at] = grad_query.astype(BF16)
        carry = carry_ref[h]
        carry_half = carry.astype(BF16)
        grad_key = dot_tn(mixed, query) + leave * dot_nt(value, carry_half)
        grad_value = dot_tn(probs_ref[0, h], grad_raw) + leave * dot_nn(key, carry_half)
        grad_key_ref[:, at] = grad_key.astype(BF16)
        grad_value_ref[:, at] = grad_value.astype(BF16)
        carry_ref[h] = keep_ref[0, 0:1, h : h + 1] * carry + dot_tn(scaled_half(query, enter), grad_raw)


def backward_local(
    queries, keys, values, raw, out_grad, gain, scale, col, row, keep, probs, states, entering, heads, size
):
    rows, width = queries.shape
    blocks = rows // BLOCK
    token = spec((BLOCK, width), lambda i: (blocks - 1 - i, 0))
    narrow = spec((BLOCK, LANES), lambda i: (blocks - 1 - i, 0))
    per_block = spec((1, heads, size, size), lambda i: (blocks - 1 - i, 0, 0, 0))
    return pl.pallas_call(
        functools.partial(backward_kernel, heads, size),
        grid=(blocks,),
        in_specs=[
            token,
            token,
            token,
            token,
            token,
            whole_spec((1, width)),
            narrow,
            narrow,
            spec((row.shape[0], BLOCK), lambda i: (0, blocks - 1 - i)),
            spec((1, 8, LANES), lambda i: (blocks - 1 - i, 0, 0)),
            per_block,
            per_block,
            whole_spec((heads, size, size)),
        ],
        out_specs=[token] * 4,
        out_shape=[jax.ShapeDtypeStruct((rows, width), BF16)] * 4,
        scratch_shapes=[pltpu.VMEM((heads, size, size), F32)],
        compiler_params=params(),
        cost_estimate=cost(16 * rows * width * size, 22 * rows * width),
        name="backward_local",
    )(queries, keys, values, raw, out_grad, gain, scale, col, row, keep, probs, states, entering)


def finish_kernel(heads, size, hops, key_ref, value_ref, grad_key_ref, grad_value_ref, col_ref, *rest):
    received, keeps = rest[:hops], rest[hops : 2 * hops - 1]
    key_out_ref, value_out_ref, beyond_ref = rest[2 * hops - 1 :]
    step = pl.program_id(0)

    @pl.when(step == 0)
    def _():
        for h in range(heads):
            beyond_ref[h] = horner(received, keeps, h).astype(BF16)

    col = col_ref[...]
    for h in range(heads):
        at = head_cols(h, size)
        leave = col[:, LEAVE_DEV * heads + h : LEAVE_DEV * heads + h + 1]
        beyond = beyond_ref[h]
        grad_key = grad_key_ref[:, at].astype(F32) + leave * dot_nt(value_ref[:, at], beyond)
        grad_value = grad_value_ref[:, at].astype(F32) + leave * dot_nn(key_ref[:, at], beyond)
        key_out_ref[:, at] = grad_key.astype(BF16)
        value_out_ref[:, at] = grad_value.astype(BF16)


def finish(keys, values, grad_key, grad_value, col, received, keeps, heads, size):
    rows, width = keys.shape
    step_rows = min(256, rows)
    token = spec((step_rows, width), lambda i: (i, 0))
    state_shape = (heads, size, size)
    return pl.pallas_call(
        functools.partial(finish_kernel, heads, size, len(received)),
        grid=(rows // step_rows,),
        in_specs=[token] * 4
        + [spec((step_rows, LANES), lambda i: (i, 0))]
        + [whole_spec(state_shape)] * len(received)
        + [whole_spec((8, LANES))] * len(keeps),
        out_specs=[token, token],
        out_shape=[jax.ShapeDtypeStruct((rows, width), BF16)] * 2,
        scratch_shapes=[pltpu.VMEM(state_shape, BF16)],
        compiler_params=params(),
        cost_estimate=cost(4 * rows * width * size, 12 * rows * width),
        name="finish",
    )(keys, values, grad_key, grad_value, col, *received, *keeps)


def from_shards(value, count, away):
    pairs = [(i, i + away) for i in range(count) if 0 <= i + away < count]
    return lax.ppermute(value, "seq", pairs)


def body(queries, keys, values, log_decay, gain, lengths, out_grad):
    rows, heads = log_decay.shape
    width = queries.shape[1]
    size = width // heads
    count = lax.axis_size("seq")
    groups = lax.axis_size("head")
    full_width = width * groups
    longest = rows * count // DOC_SHARE
    hops = max(1, min(count - 1, -(-(longest - 1) // rows)))
    first = (lax.axis_index("seq") * rows).astype(jnp.int32).reshape(1)
    gain = gain.reshape(1, width)

    state, col, row, keep, keep_dev = local_states(keys, values, log_decay, lengths, first, heads, size)
    before = [from_shards(state, count, j) for j in range(1, hops + 1)]
    keep_before = [from_shards(keep_dev, count, j) for j in range(1, hops)]
    keep_after = [from_shards(keep_dev, count, -j) for j in range(1, hops)]
    raw, probs, states = forward_local(queries, keys, values, col, row, keep, heads, size)
    raw, sums, entering = raw_and_sums(raw, queries, out_grad, gain, col, before, keep_before, heads, size)
    every = [sums] + [
        lax.ppermute(sums, "head", [(i, (i + j) % groups) for i in range(groups)]) for j in range(1, groups)
    ]
    carry, scale = carry_states(raw, queries, out_grad, gain, col, every, full_width, heads, size)
    after = [from_shards(carry, count, -j) for j in range(1, hops + 1)]
    normed, grad_query, grad_key, grad_value = backward_local(
        queries, keys, values, raw, out_grad, gain, scale, col, row, keep, probs, states, entering, heads, size
    )
    grad_key, grad_value = finish(keys, values, grad_key, grad_value, col, after, keep_after, heads, size)
    return (normed, grad_query, grad_key, grad_value)


def solution(mesh):
    token = P("seq", "head")
    in_specs = (token, token, token, token, P("head"), P(), token)
    return jax.shard_map(body, mesh=mesh, in_specs=in_specs, out_specs=(token,) * 4, check_vma=False)
```

```python
import functools

import jax
import jax.numpy as jnp
from jax import lax
from jax.experimental import pallas as pl
from jax.experimental.pallas import tpu as pltpu
from jax.sharding import PartitionSpec as P

BLOCK = 128
STEP = 512
LANES = 128
EPS = 1e-06
F32 = jnp.float32
BF16 = jnp.bfloat16
VMEM_LIMIT = 58 * 1024 * 1024
DOC_SHARE = 4


def dot_nn(left, right):
    return lax.dot_general(left, right, (((1,), (0,)), ((), ())), preferred_element_type=F32)


def dot_nt(left, right):
    return lax.dot_general(left, right, (((1,), (1,)), ((), ())), preferred_element_type=F32)


def dot_tn(left, right):
    return lax.dot_general(left, right, (((0,), (0,)), ((), ())), preferred_element_type=F32)


def head_cols(index, size):
    return slice(index * size, (index + 1) * size)


def scaled_half(array, factor):
    return (array.astype(F32) * factor).astype(BF16)


def spec(shape, index_map):
    return pl.BlockSpec(shape, index_map)


def whole_spec(shape):
    rank = len(shape)
    return pl.BlockSpec(shape, lambda i: (0,) * rank)


def params():
    return pltpu.CompilerParams(vmem_limit_bytes=VMEM_LIMIT)


def cost(flops, bytes_accessed):
    return pl.CostEstimate(flops=flops, bytes_accessed=bytes_accessed, transcendentals=0)


RUN, ENTER, LEAVE, LEAVE_DEV, DOC = range(5)
KEEP, KEEP_TO, KEEP_FROM = range(3)


def count_docs(place, ends):
    total = jnp.zeros_like(place)
    for end in ends:
        total = total + (place >= end).astype(jnp.int32)
    return total


def write_factors(heads, docs, rate_ref, len_ref, first_ref, factor_ref, keep_ref, keep_dev_ref):
    rows = rate_ref.shape[1]
    blocks = rows // BLOCK
    first = first_ref[0]
    ends, total = [], 0
    for i in range(docs):
        total = total + len_ref[i]
        ends.append(total)

    def doc_at(place):
        return jnp.where(place >= 0, count_docs(place, ends), -1)

    upper = (
        lax.broadcasted_iota(jnp.int32, (BLOCK, BLOCK), 0)
        <= lax.broadcasted_iota(jnp.int32, (BLOCK, BLOCK), 1)
    ).astype(F32)
    runs = [
        lax.dot_general(
            rate_ref[:, b * BLOCK : (b + 1) * BLOCK], upper, (((1,), (0,)), ((), ())),
            precision=lax.Precision.HIGHEST, preferred_element_type=F32,
        )
        for b in range(blocks)
    ]
    doc_before = doc_at(first - 1)
    doc_end = doc_at(first + rows - 1)
    filler = jnp.zeros((LANES - DOC * heads - 1, BLOCK), F32)
    keeps = []
    beyond = jnp.zeros((heads, 1), F32)
    for b in reversed(range(blocks)):
        at = slice(b * BLOCK, (b + 1) * BLOCK)
        start = first + b * BLOCK
        doc = count_docs(start + lax.broadcasted_iota(jnp.int32, (1, BLOCK), 1), ends)
        doc_start, doc_last = doc_at(start - 1), doc_at(start + BLOCK - 1)
        run = runs[b]
        last = run[:, BLOCK - 1 : BLOCK]
        factor_ref[RUN * heads : (RUN + 1) * heads, at] = run
        factor_ref[ENTER * heads : (ENTER + 1) * heads, at] = jnp.exp(run) * (doc == doc_start).astype(F32)
        factor_ref[LEAVE * heads : (LEAVE + 1) * heads, at] = jnp.exp(last - run) * (doc == doc_last).astype(F32)
        factor_ref[LEAVE_DEV * heads : (LEAVE_DEV + 1) * heads, at] = (
            jnp.exp(beyond + (last - run)) * (doc == doc_end).astype(F32)
        )
        factor_ref[DOC * heads : DOC * heads + 1, at] = doc.astype(F32)
        factor_ref[DOC * heads + 1 :, at] = filler
        beyond = beyond + last
        keeps.append(jnp.exp(jnp.broadcast_to(last, (heads, LANES))) * (doc_last == doc_start).astype(F32))
    keeps = keeps[::-1]
    to = jnp.ones((heads, LANES), F32)
    for b in range(blocks):
        keep_ref[b, KEEP * heads : (KEEP + 1) * heads, :] = keeps[b]
        keep_ref[b, KEEP_TO * heads : (KEEP_TO + 1) * heads, :] = to
        to = to * keeps[b]
    keep_dev_ref[...] = jnp.exp(jnp.broadcast_to(beyond, (heads, LANES))) * (doc_end == doc_before).astype(F32)
    after = jnp.ones((heads, LANES), F32)
    for b in reversed(range(blocks)):
        keep_ref[b, KEEP_FROM * heads : (KEEP_FROM + 1) * heads, :] = after
        after = after * keeps[b]


def state_kernel(
    heads, size, docs, len_ref, first_ref, rate_ref, key_ref, value_ref,
    state_ref, factor_ref, keep_ref,
):
    step = pl.program_id(0)
    rows = key_ref.shape[0]

    @pl.when(step == 0)
    def _():
        state_ref[...] = jnp.zeros_like(state_ref)
        keep_dev_ref = state_ref.at[heads * size :, :]
        write_factors(heads, docs, rate_ref, len_ref, first_ref, factor_ref, keep_ref, keep_dev_ref)

    at_rows = pl.ds(pl.multiple_of(step * rows, rows), rows)
    for h in range(heads):
        at = head_cols(h, size)
        leave = factor_ref[LEAVE_DEV * heads + h : LEAVE_DEV * heads + h + 1, at_rows]
        state_ref[state_rows(h, size), :] += dot_nn(scaled_half(key_ref[:, at].T, leave), value_ref[:, at])


def local_states(keys, values, rates, lengths, first, heads, size):
    rows, width = keys.shape
    docs = lengths.shape[0]
    step_rows = min(STEP, rows)
    blocks = rows // BLOCK
    shapes = (packed_shape(heads, size), (LANES, rows), (blocks, 3 * heads, LANES))
    smem = pl.BlockSpec(memory_space=pltpu.SMEM)
    return pl.pallas_call(
        functools.partial(state_kernel, heads, size, docs),
        grid=(rows // step_rows,),
        in_specs=[
            smem,
            smem,
            whole_spec((heads, rows)),
            spec((step_rows, width), lambda i: (i, 0)),
            spec((step_rows, width), lambda i: (i, 0)),
        ],
        out_specs=[whole_spec(s) for s in shapes],
        out_shape=[jax.ShapeDtypeStruct(s, F32) for s in shapes],
        compiler_params=params(),
        cost_estimate=cost(2 * rows * width * size, 4 * rows * width),
        name="local_state",
    )(lengths, first, rates, keys, values)


def column(col, group, heads, h):
    return col[:, group * heads + h : group * heads + h + 1]


def block_weights(heads, col, factor_ref, h, bias):
    return jnp.exp(column(col, RUN, heads, h) - factor_ref[RUN * heads + h : RUN * heads + h + 1, :] + bias)


def block_bias(heads, col, factor_ref):
    causal = lax.broadcasted_iota(jnp.int32, (BLOCK, BLOCK), 0) >= lax.broadcasted_iota(
        jnp.int32, (BLOCK, BLOCK), 1
    )
    same = column(col, DOC, heads, 0) == factor_ref[DOC * heads : DOC * heads + 1, :]
    return jnp.where(causal & same, 0.0, -1e30)


def keep_row(keep_ref, group, heads, h):
    return keep_ref[0, group * heads + h : group * heads + h + 1, :]


def forward_kernel(
    heads, size, query_ref, key_ref, value_ref, factor_ref, keep_ref,
    raw_ref, probs_ref, states_ref, query_out_ref, key_out_ref, value_out_ref, state_ref,
):
    step = pl.program_id(0)

    @pl.when(step == 0)
    def _():
        state_ref[...] = jnp.zeros_like(state_ref)

    col = factor_ref[...].T
    bias = block_bias(heads, col, factor_ref)
    for h in range(heads):
        at = head_cols(h, size)
        query, key, value = query_ref[:, at], key_ref[:, at], value_ref[:, at]
        leave = column(col, LEAVE, heads, h)
        keep_from = keep_row(keep_ref, KEEP_FROM, heads, h)
        weights = block_weights(heads, col, factor_ref, h, bias)
        probs = (dot_nt(query, key) * weights).astype(BF16)
        state = state_ref[h]
        state_half = state.astype(BF16)
        probs_ref[0, h] = probs
        states_ref[0, h] = state_half
        entered = query.astype(F32) * column(col, ENTER, heads, h)
        left = key.astype(F32) * leave
        query_out_ref[:, at] = (entered * keep_row(keep_ref, KEEP_TO, heads, h)).astype(BF16)
        key_out_ref[:, at] = (left * keep_from).astype(BF16)
        value_out_ref[:, at] = (value.astype(F32) * leave * keep_from).astype(BF16)
        both = jnp.concatenate([probs, entered.astype(BF16)], axis=1)
        raw = dot_nn(both, jnp.concatenate([value, state_half], axis=0))
        raw_ref[:, at] = raw.astype(BF16)
        state_ref[h] = keep_row(keep_ref, KEEP, heads, h) * state + dot_tn(left.astype(BF16), value)


def forward_local(queries, keys, values, factors, keep, heads, size):
    rows, width = queries.shape
    blocks = rows // BLOCK
    token = spec((BLOCK, width), lambda i: (i, 0))
    per_block = spec((1, heads, size, size), lambda i: (i, 0, 0, 0))
    token_shape = jax.ShapeDtypeStruct((rows, width), BF16)
    return pl.pallas_call(
        functools.partial(forward_kernel, heads, size),
        grid=(blocks,),
        in_specs=[
            token,
            token,
            token,
            spec((LANES, BLOCK), lambda i: (0, i)),
            spec((1,) + keep.shape[1:], lambda i: (i, 0, 0)),
        ],
        out_specs=[token, per_block, per_block, token, token, token],
        out_shape=[
            token_shape,
            jax.ShapeDtypeStruct((blocks, heads, BLOCK, BLOCK), BF16),
            jax.ShapeDtypeStruct((blocks, heads, size, size), BF16),
            token_shape,
            token_shape,
            token_shape,
        ],
        scratch_shapes=[pltpu.VMEM((heads, size, size), F32)],
        compiler_params=params(),
        cost_estimate=cost(8 * rows * width * size, 18 * rows * width),
        name="forward_local",
    )(queries, keys, values, factors, keep)


def state_rows(h, size):
    return slice(h * size, (h + 1) * size)


def entering_state(received, heads, size, h):
    keep_at = slice(heads * size + h, heads * size + h + 1)
    total = received[-1][state_rows(h, size), :]
    for packed in reversed(received[:-1]):
        total = packed[state_rows(h, size), :] + packed[keep_at, :] * total
    return total


def packed_shape(heads, size):
    return (heads * size + heads, LANES)


def raw_kernel(heads, size, hops, raw_ref, query_ref, grad_ref, gain_ref, *rest):
    received = rest[:hops]
    out_ref, sums_ref, enter_ref = rest[hops:]
    step = pl.program_id(0)
    rows = raw_ref.shape[0]

    @pl.when(step == 0)
    def _():
        for h in range(heads):
            enter_ref[h] = entering_state(received, heads, size, h).astype(BF16)

    squares = jnp.zeros((rows, size), F32)
    projected = jnp.zeros((rows, size), F32)
    for h in range(heads):
        at = head_cols(h, size)
        raw = raw_ref[:, at].astype(F32) + dot_nn(query_ref[:, at], enter_ref[h])
        out_ref[:, at] = raw.astype(BF16)
        squares = squares + raw * raw
        projected = projected + grad_ref[:, at].astype(F32) * gain_ref[:, at] * raw
    lane = lax.broadcasted_iota(jnp.int32, (rows, LANES), 1)
    packed = jnp.where(
        lane == 0,
        jnp.sum(squares, axis=1, keepdims=True),
        jnp.where(lane == 1, jnp.sum(projected, axis=1, keepdims=True), 0.0),
    )
    sums_ref[...] = packed.T[0:8, :]


def raw_and_sums(raw, queries, out_grad, gain, received, heads, size):
    rows, width = queries.shape
    step_rows = min(STEP, rows)
    token = spec((step_rows, width), lambda i: (i, 0))
    state_shape = (heads, size, size)
    return pl.pallas_call(
        functools.partial(raw_kernel, heads, size, len(received)),
        grid=(rows // step_rows,),
        in_specs=[
            token,
            token,
            token,
            whole_spec((1, width)),
        ]
        + [whole_spec(packed_shape(heads, size))] * len(received),
        out_specs=[token, spec((8, step_rows), lambda i: (0, i)), whole_spec(state_shape)],
        out_shape=[
            jax.ShapeDtypeStruct((rows, width), BF16),
            jax.ShapeDtypeStruct((8, rows), F32),
            jax.ShapeDtypeStruct(state_shape, BF16),
        ],
        compiler_params=params(),
        cost_estimate=cost(2 * rows * width * size, 8 * rows * width),
        name="raw_and_sums",
    )(raw, queries, out_grad, gain, *received)


def carry_kernel(heads, size, full_width, parts, raw_ref, query_ref, grad_ref, gain_ref, state_in_ref, *rest):
    sums = rest[:parts]
    carry_ref, scale_ref = rest[parts:]
    step = pl.program_id(0)
    rows = raw_ref.shape[0]

    @pl.when(step == 0)
    def _():
        carry_ref[...] = jnp.zeros_like(carry_ref)
        carry_ref[heads * size :, :] = state_in_ref[...]

    total = sums[0][...]
    for part in sums[1:]:
        total = total + part[...]
    total = jnp.concatenate([total, jnp.zeros((LANES - 8, rows), F32)], axis=0).T
    inverse = lax.rsqrt(total[:, 0:1] / full_width + EPS)
    slope = inverse * inverse * inverse * total[:, 1:2] / full_width
    lane = lax.broadcasted_iota(jnp.int32, (rows, LANES), 1)
    scale_ref[...] = jnp.where(lane == 0, inverse, slope)
    for h in range(heads):
        at = head_cols(h, size)
        scaled = grad_ref[:, at].astype(F32) * gain_ref[:, at]
        grad_raw = (inverse * scaled - raw_ref[:, at].astype(F32) * slope).astype(BF16)
        carry_ref[state_rows(h, size), :] += dot_tn(query_ref[:, at], grad_raw)


def carry_states(raw, queries, out_grad, gain, state, sums, full_width, heads, size):
    rows, width = queries.shape
    step_rows = min(STEP, rows)
    token = spec((step_rows, width), lambda i: (i, 0))
    narrow = spec((step_rows, LANES), lambda i: (i, 0))
    packed = packed_shape(heads, size)
    return pl.pallas_call(
        functools.partial(carry_kernel, heads, size, full_width, len(sums)),
        grid=(rows // step_rows,),
        in_specs=[token, token, token, whole_spec((1, width)), spec((heads, LANES), lambda i: (size, 0))]
        + [spec((8, step_rows), lambda i: (0, i))] * len(sums),
        out_specs=[whole_spec(packed), narrow],
        out_shape=[
            jax.ShapeDtypeStruct(packed, F32),
            jax.ShapeDtypeStruct((rows, LANES), F32),
        ],
        compiler_params=params(),
        cost_estimate=cost(2 * rows * width * size, 6 * rows * width),
        name="carry_state",
    )(raw, queries, out_grad, gain, state, *sums)


def backward_kernel(
    heads, size, query_ref, key_ref, value_ref, raw_ref, out_grad_ref, gain_ref, scale_ref,
    factor_ref, keep_ref, probs_ref, states_ref, enter_ref,
    normed_ref, grad_query_ref, grad_key_ref, grad_value_ref, carry_ref,
):
    step = pl.program_id(0)

    @pl.when(step == 0)
    def _():
        carry_ref[...] = jnp.zeros_like(carry_ref)

    col = factor_ref[...].T
    bias = block_bias(heads, col, factor_ref)
    inverse, slope = scale_ref[:, 0:1], scale_ref[:, 1:2]
    for h in range(heads):
        at = head_cols(h, size)
        query, key, value = query_ref[:, at], key_ref[:, at], value_ref[:, at]
        raw, gain = raw_ref[:, at].astype(F32), gain_ref[:, at]
        enter, leave = column(col, ENTER, heads, h), column(col, LEAVE, heads, h)
        grad_raw = (inverse * (out_grad_ref[:, at].astype(F32) * gain) - raw * slope).astype(BF16)
        normed_ref[:, at] = (raw * inverse * gain).astype(BF16)
        weights = block_weights(heads, col, factor_ref, h, bias)
        mixed = (dot_nt(grad_raw, value) * weights).astype(BF16)
        prefix = keep_row(keep_ref, KEEP_TO, heads, h)
        state = (states_ref[0, h].astype(F32) + prefix * enter_ref[h].astype(F32)).astype(BF16)
        grad_query = dot_nn(mixed, key) + enter * dot_nt(grad_raw, state)
        grad_query_ref[:, at] = grad_query.astype(BF16)
        carry = carry_ref[h]
        carry_half = carry.astype(BF16)
        grad_key = dot_tn(mixed, query) + leave * dot_nt(value, carry_half)
        grad_value = dot_tn(probs_ref[0, h], grad_raw) + leave * dot_nn(key, carry_half)
        grad_key_ref[:, at] = grad_key.astype(BF16)
        grad_value_ref[:, at] = grad_value.astype(BF16)
        enter_row = factor_ref[ENTER * heads + h : ENTER * heads + h + 1, :]
        update = dot_nn(scaled_half(query.T, enter_row), grad_raw)
        carry_ref[h] = keep_row(keep_ref, KEEP, heads, h) * carry + update


def backward_local(
    queries, keys, values, raw, out_grad, gain, scale, factors, keep, probs, states, entering, heads, size
):
    rows, width = queries.shape
    blocks = rows // BLOCK
    token = spec((BLOCK, width), lambda i: (blocks - 1 - i, 0))
    narrow = spec((BLOCK, LANES), lambda i: (blocks - 1 - i, 0))
    per_block = spec((1, heads, size, size), lambda i: (blocks - 1 - i, 0, 0, 0))
    return pl.pallas_call(
        functools.partial(backward_kernel, heads, size),
        grid=(blocks,),
        in_specs=[
            token,
            token,
            token,
            token,
            token,
            whole_spec((1, width)),
            narrow,
            spec((LANES, BLOCK), lambda i: (0, blocks - 1 - i)),
            spec((1,) + keep.shape[1:], lambda i: (blocks - 1 - i, 0, 0)),
            per_block,
            per_block,
            whole_spec((heads, size, size)),
        ],
        out_specs=[token] * 4,
        out_shape=[jax.ShapeDtypeStruct((rows, width), BF16)] * 4,
        scratch_shapes=[pltpu.VMEM((heads, size, size), F32)],
        compiler_params=params(),
        cost_estimate=cost(16 * rows * width * size, 22 * rows * width),
        name="backward_local",
    )(queries, keys, values, raw, out_grad, gain, scale, factors, keep, probs, states, entering)


def finish_kernel(heads, size, hops, key_ref, value_ref, grad_key_ref, grad_value_ref, *rest):
    received = rest[:hops]
    key_out_ref, value_out_ref, beyond_ref = rest[hops:]
    step = pl.program_id(0)

    @pl.when(step == 0)
    def _():
        for h in range(heads):
            beyond_ref[h] = entering_state(received, heads, size, h).astype(BF16)

    for h in range(heads):
        at = head_cols(h, size)
        beyond = beyond_ref[h]
        grad_key = grad_key_ref[:, at].astype(F32) + dot_nt(value_ref[:, at], beyond)
        grad_value = grad_value_ref[:, at].astype(F32) + dot_nn(key_ref[:, at], beyond)
        key_out_ref[:, at] = grad_key.astype(BF16)
        value_out_ref[:, at] = grad_value.astype(BF16)


def finish(keys, values, grad_key, grad_value, received, heads, size):
    rows, width = keys.shape
    step_rows = min(STEP, rows)
    token = spec((step_rows, width), lambda i: (i, 0))
    return pl.pallas_call(
        functools.partial(finish_kernel, heads, size, len(received)),
        grid=(rows // step_rows,),
        in_specs=[token] * 4
        + [whole_spec(packed_shape(heads, size))] * len(received),
        out_specs=[token, token],
        out_shape=[jax.ShapeDtypeStruct((rows, width), BF16)] * 2,
        scratch_shapes=[pltpu.VMEM((heads, size, size), BF16)],
        compiler_params=params(),
        cost_estimate=cost(4 * rows * width * size, 12 * rows * width),
        name="finish",
    )(keys, values, grad_key, grad_value, *received)


def from_shards(value, count, away):
    pairs = [(i, i + away) for i in range(count) if 0 <= i + away < count]
    return lax.ppermute(value, "seq", pairs)


def body(queries, keys, values, log_decay, gain, lengths, out_grad):
    rows, heads = log_decay.shape
    width = queries.shape[1]
    size = width // heads
    count = lax.axis_size("seq")
    groups = lax.axis_size("head")
    full_width = width * groups
    longest = rows * count // DOC_SHARE
    hops = max(1, min(count - 1, -(-(longest - 1) // rows)))
    first = (lax.axis_index("seq") * rows).astype(jnp.int32).reshape(1)
    gain = gain.reshape(1, width)

    state, factors, keep = local_states(keys, values, log_decay.T, lengths, first, heads, size)
    before = [from_shards(state, count, j) for j in range(1, hops + 1)]
    raw, probs, states, query_in, key_out, value_out = forward_local(
        queries, keys, values, factors, keep, heads, size
    )
    raw, sums, entering = raw_and_sums(raw, query_in, out_grad, gain, before, heads, size)
    every = [sums] + [
        lax.ppermute(sums, "head", [(i, (i + j) % groups) for i in range(groups)]) for j in range(1, groups)
    ]
    carry, scale = carry_states(raw, query_in, out_grad, gain, state, every, full_width, heads, size)
    after = [from_shards(carry, count, -j) for j in range(1, hops + 1)]
    normed, grad_query, grad_key, grad_value = backward_local(
        queries, keys, values, raw, out_grad, gain, scale, factors, keep, probs, states, entering, heads, size
    )
    grad_key, grad_value = finish(key_out, value_out, grad_key, grad_value, after, heads, size)
    return (normed, grad_query, grad_key, grad_value)


def solution(mesh):
    token = P("seq", "head")
    in_specs = (token, token, token, token, P("head"), P(), token)
    return jax.shard_map(body, mesh=mesh, in_specs=in_specs, out_specs=(token,) * 4, check_vma=False)
```

```python
import functools

import jax
import jax.numpy as jnp
from jax import lax
from jax.experimental import pallas as pl
from jax.experimental.pallas import tpu as pltpu
from jax.sharding import PartitionSpec as P

BLOCK = 128
STEP = 512
LANES = 128
EPS = 1e-06
F32 = jnp.float32
BF16 = jnp.bfloat16
VMEM_LIMIT = 58 * 1024 * 1024
DOC_SHARE = 4


def dot_nn(left, right):
    return lax.dot_general(left, right, (((1,), (0,)), ((), ())), preferred_element_type=F32)


def dot_nt(left, right):
    return lax.dot_general(left, right, (((1,), (1,)), ((), ())), preferred_element_type=F32)


def dot_tn(left, right):
    return lax.dot_general(left, right, (((0,), (0,)), ((), ())), preferred_element_type=F32)


def head_cols(index, size):
    return slice(index * size, (index + 1) * size)


def scaled_half(array, factor):
    return (array.astype(F32) * factor).astype(BF16)


def spec(shape, index_map):
    return pl.BlockSpec(shape, index_map)


def whole_spec(shape):
    rank = len(shape)
    return pl.BlockSpec(shape, lambda i: (0,) * rank)


def params():
    return pltpu.CompilerParams(vmem_limit_bytes=VMEM_LIMIT)


def cost(flops, bytes_accessed):
    return pl.CostEstimate(flops=flops, bytes_accessed=bytes_accessed, transcendentals=0)


RUN, ENTER, LEAVE, LEAVE_DEV, DOC = range(5)
KEEP, KEEP_TO, KEEP_FROM = range(3)


def count_docs(place, ends):
    total = jnp.zeros_like(place)
    for end in ends:
        total = total + (place >= end).astype(jnp.int32)
    return total


def write_covered(count, rows, ends, covered_ref):
    found = [0, 0]
    for i in range(count):
        at_edge = 0
        for end in ends:
            at_edge = at_edge + ((end >= i * rows) & (end <= (i + 1) * rows)).astype(jnp.int32)
        found[i % 2] = found[i % 2] + (at_edge == 0).astype(jnp.int32)
    for parity in range(2):
        covered_ref[parity] = jnp.minimum(found[parity], 1)


def write_factors(heads, docs, count, rate_ref, len_ref, first_ref, factor_ref, keep_ref, keep_dev_ref, covered_ref):
    rows = rate_ref.shape[1]
    blocks = rows // BLOCK
    first = first_ref[0]
    ends, total = [], 0
    for i in range(docs):
        total = total + len_ref[i]
        ends.append(total)
    write_covered(count, rows, ends, covered_ref)

    def doc_at(place):
        return jnp.where(place >= 0, count_docs(place, ends), -1)

    upper = (
        lax.broadcasted_iota(jnp.int32, (BLOCK, BLOCK), 0)
        <= lax.broadcasted_iota(jnp.int32, (BLOCK, BLOCK), 1)
    ).astype(F32)
    runs = [
        lax.dot_general(
            rate_ref[:, b * BLOCK : (b + 1) * BLOCK], upper, (((1,), (0,)), ((), ())),
            precision=lax.Precision.HIGHEST, preferred_element_type=F32,
        )
        for b in range(blocks)
    ]
    doc_before = doc_at(first - 1)
    doc_end = doc_at(first + rows - 1)
    filler = jnp.zeros((LANES - DOC * heads - 1, BLOCK), F32)
    keeps = []
    beyond = jnp.zeros((heads, 1), F32)
    for b in reversed(range(blocks)):
        at = slice(b * BLOCK, (b + 1) * BLOCK)
        start = first + b * BLOCK
        doc = count_docs(start + lax.broadcasted_iota(jnp.int32, (1, BLOCK), 1), ends)
        doc_start, doc_last = doc_at(start - 1), doc_at(start + BLOCK - 1)
        run = runs[b]
        last = run[:, BLOCK - 1 : BLOCK]
        factor_ref[RUN * heads : (RUN + 1) * heads, at] = run
        factor_ref[ENTER * heads : (ENTER + 1) * heads, at] = jnp.exp(run) * (doc == doc_start).astype(F32)
        factor_ref[LEAVE * heads : (LEAVE + 1) * heads, at] = jnp.exp(last - run) * (doc == doc_last).astype(F32)
        factor_ref[LEAVE_DEV * heads : (LEAVE_DEV + 1) * heads, at] = (
            jnp.exp(beyond + (last - run)) * (doc == doc_end).astype(F32)
        )
        factor_ref[DOC * heads : DOC * heads + 1, at] = doc.astype(F32)
        factor_ref[DOC * heads + 1 :, at] = filler
        beyond = beyond + last
        keeps.append(jnp.exp(jnp.broadcast_to(last, (heads, LANES))) * (doc_last == doc_start).astype(F32))
    keeps = keeps[::-1]
    to = jnp.ones((heads, LANES), F32)
    for b in range(blocks):
        keep_ref[b, KEEP * heads : (KEEP + 1) * heads, :] = keeps[b]
        keep_ref[b, KEEP_TO * heads : (KEEP_TO + 1) * heads, :] = to
        to = to * keeps[b]
    keep_dev_ref[...] = jnp.exp(jnp.broadcast_to(beyond, (heads, LANES))) * (doc_end == doc_before).astype(F32)
    after = jnp.ones((heads, LANES), F32)
    for b in reversed(range(blocks)):
        keep_ref[b, KEEP_FROM * heads : (KEEP_FROM + 1) * heads, :] = after
        after = after * keeps[b]


def state_kernel(
    heads, size, docs, count, len_ref, first_ref, rate_ref, key_ref, value_ref,
    state_ref, factor_ref, keep_ref, covered_ref,
):
    step = pl.program_id(0)
    rows = key_ref.shape[0]

    @pl.when(step == 0)
    def _():
        state_ref[...] = jnp.zeros_like(state_ref)
        keep_dev_ref = state_ref.at[heads * size :, :]
        write_factors(
            heads, docs, count, rate_ref, len_ref, first_ref, factor_ref, keep_ref, keep_dev_ref, covered_ref
        )

    at_rows = pl.ds(pl.multiple_of(step * rows, rows), rows)
    for h in range(heads):
        at = head_cols(h, size)
        leave = factor_ref[LEAVE_DEV * heads + h : LEAVE_DEV * heads + h + 1, at_rows]
        state_ref[state_rows(h, size), :] += dot_nn(scaled_half(key_ref[:, at].T, leave), value_ref[:, at])


def local_states(keys, values, rates, lengths, first, count, heads, size):
    rows, width = keys.shape
    docs = lengths.shape[0]
    step_rows = min(STEP, rows)
    blocks = rows // BLOCK
    shapes = (packed_shape(heads, size), (LANES, rows), (blocks, 3 * heads, LANES))
    smem = pl.BlockSpec(memory_space=pltpu.SMEM)
    return pl.pallas_call(
        functools.partial(state_kernel, heads, size, docs, count),
        grid=(rows // step_rows,),
        in_specs=[
            smem,
            smem,
            whole_spec((heads, rows)),
            spec((step_rows, width), lambda i: (i, 0)),
            spec((step_rows, width), lambda i: (i, 0)),
        ],
        out_specs=[whole_spec(s) for s in shapes] + [smem],
        out_shape=[jax.ShapeDtypeStruct(s, F32) for s in shapes] + [jax.ShapeDtypeStruct((2,), jnp.int32)],
        compiler_params=params(),
        cost_estimate=cost(2 * rows * width * size, 4 * rows * width),
        name="local_state",
    )(lengths, first, rates, keys, values)


def column(col, group, heads, h):
    return col[:, group * heads + h : group * heads + h + 1]


def block_weights(heads, col, factor_ref, h, bias):
    return jnp.exp(column(col, RUN, heads, h) - factor_ref[RUN * heads + h : RUN * heads + h + 1, :] + bias)


def block_bias(heads, col, factor_ref):
    causal = lax.broadcasted_iota(jnp.int32, (BLOCK, BLOCK), 0) >= lax.broadcasted_iota(
        jnp.int32, (BLOCK, BLOCK), 1
    )
    same = column(col, DOC, heads, 0) == factor_ref[DOC * heads : DOC * heads + 1, :]
    return jnp.where(causal & same, 0.0, -1e30)


def keep_row(keep_ref, group, heads, h):
    return keep_ref[0, group * heads + h : group * heads + h + 1, :]


def forward_kernel(
    heads, size, query_ref, key_ref, value_ref, factor_ref, keep_ref,
    raw_ref, probs_ref, states_ref, query_out_ref, key_out_ref, value_out_ref, state_ref,
):
    step = pl.program_id(0)

    @pl.when(step == 0)
    def _():
        state_ref[...] = jnp.zeros_like(state_ref)

    col = factor_ref[...].T
    bias = block_bias(heads, col, factor_ref)
    for h in range(heads):
        at = head_cols(h, size)
        query, key, value = query_ref[:, at], key_ref[:, at], value_ref[:, at]
        leave = column(col, LEAVE, heads, h)
        keep_from = keep_row(keep_ref, KEEP_FROM, heads, h)
        weights = block_weights(heads, col, factor_ref, h, bias)
        probs = (dot_nt(query, key) * weights).astype(BF16)
        state = state_ref[h]
        state_half = state.astype(BF16)
        probs_ref[0, h] = probs
        states_ref[0, h] = state_half
        entered = query.astype(F32) * column(col, ENTER, heads, h)
        left = key.astype(F32) * leave
        query_out_ref[:, at] = (entered * keep_row(keep_ref, KEEP_TO, heads, h)).astype(BF16)
        key_out_ref[:, at] = (left * keep_from).astype(BF16)
        value_out_ref[:, at] = (value.astype(F32) * leave * keep_from).astype(BF16)
        both = jnp.concatenate([probs, entered.astype(BF16)], axis=1)
        raw = dot_nn(both, jnp.concatenate([value, state_half], axis=0))
        raw_ref[:, at] = raw.astype(BF16)
        state_ref[h] = keep_row(keep_ref, KEEP, heads, h) * state + dot_tn(left.astype(BF16), value)


def forward_local(queries, keys, values, factors, keep, heads, size):
    rows, width = queries.shape
    blocks = rows // BLOCK
    token = spec((BLOCK, width), lambda i: (i, 0))
    per_block = spec((1, heads, size, size), lambda i: (i, 0, 0, 0))
    token_shape = jax.ShapeDtypeStruct((rows, width), BF16)
    return pl.pallas_call(
        functools.partial(forward_kernel, heads, size),
        grid=(blocks,),
        in_specs=[
            token,
            token,
            token,
            spec((LANES, BLOCK), lambda i: (0, i)),
            spec((1,) + keep.shape[1:], lambda i: (i, 0, 0)),
        ],
        out_specs=[token, per_block, per_block, token, token, token],
        out_shape=[
            token_shape,
            jax.ShapeDtypeStruct((blocks, heads, BLOCK, BLOCK), BF16),
            jax.ShapeDtypeStruct((blocks, heads, size, size), BF16),
            token_shape,
            token_shape,
            token_shape,
        ],
        scratch_shapes=[pltpu.VMEM((heads, size, size), F32)],
        compiler_params=params(),
        cost_estimate=cost(8 * rows * width * size, 18 * rows * width),
        name="forward_local",
    )(queries, keys, values, factors, keep)


def state_rows(h, size):
    return slice(h * size, (h + 1) * size)


def entering_state(received, heads, size, h):
    keep_at = slice(heads * size + h, heads * size + h + 1)
    total = received[-1][state_rows(h, size), :]
    for packed in reversed(received[:-1]):
        total = packed[state_rows(h, size), :] + packed[keep_at, :] * total
    return total


def packed_shape(heads, size):
    return (heads * size + heads, LANES)


def raw_kernel(heads, size, hops, raw_ref, query_ref, grad_ref, gain_ref, *rest):
    received = rest[:hops]
    out_ref, sums_ref, enter_ref = rest[hops:]
    step = pl.program_id(0)
    rows = raw_ref.shape[0]

    @pl.when(step == 0)
    def _():
        for h in range(heads):
            enter_ref[h] = entering_state(received, heads, size, h).astype(BF16)

    squares = jnp.zeros((rows, size), F32)
    projected = jnp.zeros((rows, size), F32)
    for h in range(heads):
        at = head_cols(h, size)
        raw = raw_ref[:, at].astype(F32) + dot_nn(query_ref[:, at], enter_ref[h])
        out_ref[:, at] = raw.astype(BF16)
        squares = squares + raw * raw
        projected = projected + grad_ref[:, at].astype(F32) * gain_ref[:, at] * raw
    lane = lax.broadcasted_iota(jnp.int32, (rows, LANES), 1)
    packed = jnp.where(
        lane == 0,
        jnp.sum(squares, axis=1, keepdims=True),
        jnp.where(lane == 1, jnp.sum(projected, axis=1, keepdims=True), 0.0),
    )
    sums_ref[...] = packed.T[0:8, :]


def raw_and_sums(raw, queries, out_grad, gain, received, heads, size):
    rows, width = queries.shape
    step_rows = min(STEP, rows)
    token = spec((step_rows, width), lambda i: (i, 0))
    state_shape = (heads, size, size)
    return pl.pallas_call(
        functools.partial(raw_kernel, heads, size, len(received)),
        grid=(rows // step_rows,),
        in_specs=[
            token,
            token,
            token,
            whole_spec((1, width)),
        ]
        + [whole_spec(packed_shape(heads, size))] * len(received),
        out_specs=[token, spec((8, step_rows), lambda i: (0, i)), whole_spec(state_shape)],
        out_shape=[
            jax.ShapeDtypeStruct((rows, width), BF16),
            jax.ShapeDtypeStruct((8, rows), F32),
            jax.ShapeDtypeStruct(state_shape, BF16),
        ],
        compiler_params=params(),
        cost_estimate=cost(2 * rows * width * size, 8 * rows * width),
        name="raw_and_sums",
    )(raw, queries, out_grad, gain, *received)


def carry_kernel(heads, size, full_width, parts, raw_ref, query_ref, grad_ref, gain_ref, state_in_ref, *rest):
    sums = rest[:parts]
    carry_ref, scale_ref = rest[parts:]
    step = pl.program_id(0)
    rows = raw_ref.shape[0]

    @pl.when(step == 0)
    def _():
        carry_ref[...] = jnp.zeros_like(carry_ref)
        carry_ref[heads * size :, :] = state_in_ref[...]

    total = sums[0][...]
    for part in sums[1:]:
        total = total + part[...]
    total = jnp.concatenate([total, jnp.zeros((LANES - 8, rows), F32)], axis=0).T
    inverse = lax.rsqrt(total[:, 0:1] / full_width + EPS)
    slope = inverse * inverse * inverse * total[:, 1:2] / full_width
    lane = lax.broadcasted_iota(jnp.int32, (rows, LANES), 1)
    scale_ref[...] = jnp.where(lane == 0, inverse, slope)
    for h in range(heads):
        at = head_cols(h, size)
        scaled = grad_ref[:, at].astype(F32) * gain_ref[:, at]
        grad_raw = (inverse * scaled - raw_ref[:, at].astype(F32) * slope).astype(BF16)
        carry_ref[state_rows(h, size), :] += dot_tn(query_ref[:, at], grad_raw)


def carry_states(raw, queries, out_grad, gain, state, sums, full_width, heads, size):
    rows, width = queries.shape
    step_rows = min(STEP, rows)
    token = spec((step_rows, width), lambda i: (i, 0))
    narrow = spec((step_rows, LANES), lambda i: (i, 0))
    packed = packed_shape(heads, size)
    return pl.pallas_call(
        functools.partial(carry_kernel, heads, size, full_width, len(sums)),
        grid=(rows // step_rows,),
        in_specs=[token, token, token, whole_spec((1, width)), spec((heads, LANES), lambda i: (size, 0))]
        + [spec((8, step_rows), lambda i: (0, i))] * len(sums),
        out_specs=[whole_spec(packed), narrow],
        out_shape=[
            jax.ShapeDtypeStruct(packed, F32),
            jax.ShapeDtypeStruct((rows, LANES), F32),
        ],
        compiler_params=params(),
        cost_estimate=cost(2 * rows * width * size, 6 * rows * width),
        name="carry_state",
    )(raw, queries, out_grad, gain, state, *sums)


def backward_kernel(
    heads, size, query_ref, key_ref, value_ref, raw_ref, out_grad_ref, gain_ref, scale_ref,
    factor_ref, keep_ref, probs_ref, states_ref, enter_ref,
    normed_ref, grad_query_ref, grad_key_ref, grad_value_ref, carry_ref,
):
    step = pl.program_id(0)

    @pl.when(step == 0)
    def _():
        carry_ref[...] = jnp.zeros_like(carry_ref)

    col = factor_ref[...].T
    bias = block_bias(heads, col, factor_ref)
    inverse, slope = scale_ref[:, 0:1], scale_ref[:, 1:2]
    for h in range(heads):
        at = head_cols(h, size)
        query, key, value = query_ref[:, at], key_ref[:, at], value_ref[:, at]
        raw, gain = raw_ref[:, at].astype(F32), gain_ref[:, at]
        enter, leave = column(col, ENTER, heads, h), column(col, LEAVE, heads, h)
        grad_raw = (inverse * (out_grad_ref[:, at].astype(F32) * gain) - raw * slope).astype(BF16)
        normed_ref[:, at] = (raw * inverse * gain).astype(BF16)
        weights = block_weights(heads, col, factor_ref, h, bias)
        mixed = (dot_nt(grad_raw, value) * weights).astype(BF16)
        prefix = keep_row(keep_ref, KEEP_TO, heads, h)
        state = (states_ref[0, h].astype(F32) + prefix * enter_ref[h].astype(F32)).astype(BF16)
        grad_query = dot_nn(mixed, key) + enter * dot_nt(grad_raw, state)
        grad_query_ref[:, at] = grad_query.astype(BF16)
        carry = carry_ref[h]
        carry_half = carry.astype(BF16)
        grad_key = dot_tn(mixed, query) + leave * dot_nt(value, carry_half)
        grad_value = dot_tn(probs_ref[0, h], grad_raw) + leave * dot_nn(key, carry_half)
        grad_key_ref[:, at] = grad_key.astype(BF16)
        grad_value_ref[:, at] = grad_value.astype(BF16)
        enter_row = factor_ref[ENTER * heads + h : ENTER * heads + h + 1, :]
        update = dot_nn(scaled_half(query.T, enter_row), grad_raw)
        carry_ref[h] = keep_row(keep_ref, KEEP, heads, h) * carry + update


def backward_local(
    queries, keys, values, raw, out_grad, gain, scale, factors, keep, probs, states, entering, heads, size
):
    rows, width = queries.shape
    blocks = rows // BLOCK
    token = spec((BLOCK, width), lambda i: (blocks - 1 - i, 0))
    narrow = spec((BLOCK, LANES), lambda i: (blocks - 1 - i, 0))
    per_block = spec((1, heads, size, size), lambda i: (blocks - 1 - i, 0, 0, 0))
    return pl.pallas_call(
        functools.partial(backward_kernel, heads, size),
        grid=(blocks,),
        in_specs=[
            token,
            token,
            token,
            token,
            token,
            whole_spec((1, width)),
            narrow,
            spec((LANES, BLOCK), lambda i: (0, blocks - 1 - i)),
            spec((1,) + keep.shape[1:], lambda i: (blocks - 1 - i, 0, 0)),
            per_block,
            per_block,
            whole_spec((heads, size, size)),
        ],
        out_specs=[token] * 4,
        out_shape=[jax.ShapeDtypeStruct((rows, width), BF16)] * 4,
        scratch_shapes=[pltpu.VMEM((heads, size, size), F32)],
        compiler_params=params(),
        cost_estimate=cost(16 * rows * width * size, 22 * rows * width),
        name="backward_local",
    )(queries, keys, values, raw, out_grad, gain, scale, factors, keep, probs, states, entering)


def finish_kernel(heads, size, hops, key_ref, value_ref, grad_key_ref, grad_value_ref, *rest):
    received = rest[:hops]
    key_out_ref, value_out_ref, beyond_ref = rest[hops:]
    step = pl.program_id(0)

    @pl.when(step == 0)
    def _():
        for h in range(heads):
            beyond_ref[h] = entering_state(received, heads, size, h).astype(BF16)

    for h in range(heads):
        at = head_cols(h, size)
        beyond = beyond_ref[h]
        grad_key = grad_key_ref[:, at].astype(F32) + dot_nt(value_ref[:, at], beyond)
        grad_value = grad_value_ref[:, at].astype(F32) + dot_nn(key_ref[:, at], beyond)
        key_out_ref[:, at] = grad_key.astype(BF16)
        value_out_ref[:, at] = grad_value.astype(BF16)


def finish(keys, values, grad_key, grad_value, received, heads, size):
    rows, width = keys.shape
    step_rows = min(STEP, rows)
    token = spec((step_rows, width), lambda i: (i, 0))
    return pl.pallas_call(
        functools.partial(finish_kernel, heads, size, len(received)),
        grid=(rows // step_rows,),
        in_specs=[token] * 4
        + [whole_spec(packed_shape(heads, size))] * len(received),
        out_specs=[token, token],
        out_shape=[jax.ShapeDtypeStruct((rows, width), BF16)] * 2,
        scratch_shapes=[pltpu.VMEM((heads, size, size), BF16)],
        compiler_params=params(),
        cost_estimate=cost(4 * rows * width * size, 12 * rows * width),
        name="finish",
    )(keys, values, grad_key, grad_value, *received)


def send_on(value, count, hops, towards, senders):
    received = []
    for j in range(1, hops + 1):
        ahead = towards * j
        pairs = [(i, i + ahead) for i in range(count) if 0 <= i + ahead < count and (j == 1 or i in senders[j])]
        received.append(lax.ppermute(value, "seq", pairs) if pairs else jnp.zeros_like(value))
    return received


def exchange(value, count, hops, towards, parity, crowded, local):
    everyone = {j: range(count) for j in range(2, hops + 1)}
    some = {j: range(parity, count, 2) if j == 2 else () for j in range(2, hops + 1)}

    def branch(senders):
        def run(value):
            received = send_on(value, count, hops, towards, senders)
            return received, local()

        return run

    if hops == 1:
        return branch({})(value)
    return lax.switch(crowded, [branch(some), branch(everyone)], value)


def body(queries, keys, values, log_decay, gain, lengths, out_grad):
    rows, heads = log_decay.shape
    width = queries.shape[1]
    size = width // heads
    count = lax.axis_size("seq")
    groups = lax.axis_size("head")
    full_width = width * groups
    longest = rows * count // DOC_SHARE
    hops = max(1, min(count - 1, -(-(longest - 1) // rows)))
    first = (lax.axis_index("seq") * rows).astype(jnp.int32).reshape(1)
    gain = gain.reshape(1, width)

    state, factors, keep, covered = local_states(
        keys, values, log_decay.T, lengths, first, count, heads, size
    )
    before, (raw, probs, states, query_in, key_out, value_out) = exchange(
        state, count, hops, 1, 0, covered[0],
        lambda: forward_local(queries, keys, values, factors, keep, heads, size),
    )
    raw, sums, entering = raw_and_sums(raw, query_in, out_grad, gain, before, heads, size)
    every = [sums] + [
        lax.ppermute(sums, "head", [(i, (i + j) % groups) for i in range(groups)]) for j in range(1, groups)
    ]
    carry, scale = carry_states(raw, query_in, out_grad, gain, state, every, full_width, heads, size)
    after, (normed, grad_query, grad_key, grad_value) = exchange(
        carry, count, hops, -1, 1, covered[1],
        lambda: backward_local(
            queries, keys, values, raw, out_grad, gain, scale, factors, keep, probs, states, entering, heads, size
        ),
    )
    grad_key, grad_value = finish(key_out, value_out, grad_key, grad_value, after, heads, size)
    return (normed, grad_query, grad_key, grad_value)


def solution(mesh):
    token = P("seq", "head")
    in_specs = (token, token, token, token, P("head"), P(), token)
    return jax.shard_map(body, mesh=mesh, in_specs=in_specs, out_specs=(token,) * 4, check_vma=False)
```

```python
import functools

import jax
import jax.numpy as jnp
from jax import lax
from jax.experimental import pallas as pl
from jax.experimental.pallas import tpu as pltpu
from jax.sharding import PartitionSpec as P

BLOCK = 128
LANES = 128
EPS = 1e-06
F32 = jnp.float32
BF16 = jnp.bfloat16
ROWS_AND_VMEM = {
    "local_state": (512, 58),
    "forward_local": (BLOCK, 14),
    "raw_and_sums": (256, 14),
    "carry_state": (256, 14),
    "backward_local": (BLOCK, 16),
    "finish": (256, 18),
}
DOC_SHARE = 4


def dot_nn(left, right):
    return lax.dot_general(left, right, (((1,), (0,)), ((), ())), preferred_element_type=F32)


def dot_nt(left, right):
    return lax.dot_general(left, right, (((1,), (1,)), ((), ())), preferred_element_type=F32)


def dot_tn(left, right):
    return lax.dot_general(left, right, (((0,), (0,)), ((), ())), preferred_element_type=F32)


def head_cols(index, size):
    return slice(index * size, (index + 1) * size)


def scaled_half(array, factor):
    return (array.astype(F32) * factor).astype(BF16)


def spec(shape, index_map):
    return pl.BlockSpec(shape, index_map)


def whole_spec(shape):
    rank = len(shape)
    return pl.BlockSpec(shape, lambda i: (0,) * rank)


def params(name):
    return pltpu.CompilerParams(vmem_limit_bytes=ROWS_AND_VMEM[name][1] * 1024 * 1024)


def cost(flops, bytes_accessed):
    return pl.CostEstimate(flops=flops, bytes_accessed=bytes_accessed, transcendentals=0)


RUN, ENTER, LEAVE, LEAVE_DEV, DOC = range(5)
KEEP, KEEP_TO, KEEP_FROM = range(3)


def count_docs(place, ends):
    total = jnp.zeros_like(place)
    for end in ends:
        total = total + (place >= end).astype(jnp.int32)
    return total


def write_covered(count, rows, ends, covered_ref):
    found = [0, 0]
    for i in range(count):
        at_edge = 0
        for end in ends:
            at_edge = at_edge + ((end >= i * rows) & (end <= (i + 1) * rows)).astype(jnp.int32)
        found[i % 2] = found[i % 2] + (at_edge == 0).astype(jnp.int32)
    for parity in range(2):
        covered_ref[parity] = jnp.minimum(found[parity], 1)


def write_factors(heads, docs, count, rate_ref, len_ref, first_ref, factor_ref, keep_ref, keep_dev_ref, covered_ref):
    rows = rate_ref.shape[1]
    blocks = rows // BLOCK
    first = first_ref[0]
    ends, total = [], 0
    for i in range(docs):
        total = total + len_ref[i]
        ends.append(total)
    write_covered(count, rows, ends, covered_ref)

    def doc_at(place):
        return jnp.where(place >= 0, count_docs(place, ends), -1)

    upper = (
        lax.broadcasted_iota(jnp.int32, (BLOCK, BLOCK), 0)
        <= lax.broadcasted_iota(jnp.int32, (BLOCK, BLOCK), 1)
    ).astype(F32)
    runs = [
        lax.dot_general(
            rate_ref[:, b * BLOCK : (b + 1) * BLOCK], upper, (((1,), (0,)), ((), ())),
            precision=lax.Precision.HIGHEST, preferred_element_type=F32,
        )
        for b in range(blocks)
    ]
    doc_before = doc_at(first - 1)
    doc_end = doc_at(first + rows - 1)
    filler = jnp.zeros((LANES - DOC * heads - 1, BLOCK), F32)
    keeps = []
    beyond = jnp.zeros((heads, 1), F32)
    for b in reversed(range(blocks)):
        at = slice(b * BLOCK, (b + 1) * BLOCK)
        start = first + b * BLOCK
        doc = count_docs(start + lax.broadcasted_iota(jnp.int32, (1, BLOCK), 1), ends)
        doc_start, doc_last = doc_at(start - 1), doc_at(start + BLOCK - 1)
        run = runs[b]
        last = run[:, BLOCK - 1 : BLOCK]
        factor_ref[RUN * heads : (RUN + 1) * heads, at] = run
        factor_ref[ENTER * heads : (ENTER + 1) * heads, at] = jnp.exp(run) * (doc == doc_start).astype(F32)
        factor_ref[LEAVE * heads : (LEAVE + 1) * heads, at] = jnp.exp(last - run) * (doc == doc_last).astype(F32)
        factor_ref[LEAVE_DEV * heads : (LEAVE_DEV + 1) * heads, at] = (
            jnp.exp(beyond + (last - run)) * (doc == doc_end).astype(F32)
        )
        factor_ref[DOC * heads : DOC * heads + 1, at] = doc.astype(F32)
        factor_ref[DOC * heads + 1 :, at] = filler
        beyond = beyond + last
        keeps.append(jnp.exp(jnp.broadcast_to(last, (heads, LANES))) * (doc_last == doc_start).astype(F32))
    keeps = keeps[::-1]
    to = jnp.ones((heads, LANES), F32)
    for b in range(blocks):
        keep_ref[b, KEEP * heads : (KEEP + 1) * heads, :] = keeps[b]
        keep_ref[b, KEEP_TO * heads : (KEEP_TO + 1) * heads, :] = to
        to = to * keeps[b]
    keep_dev_ref[...] = jnp.exp(jnp.broadcast_to(beyond, (heads, LANES))) * (doc_end == doc_before).astype(F32)
    after = jnp.ones((heads, LANES), F32)
    for b in reversed(range(blocks)):
        keep_ref[b, KEEP_FROM * heads : (KEEP_FROM + 1) * heads, :] = after
        after = after * keeps[b]


def state_kernel(
    heads, size, docs, count, len_ref, first_ref, rate_ref, key_ref, value_ref,
    state_ref, factor_ref, keep_ref, covered_ref,
):
    step = pl.program_id(0)
    rows = key_ref.shape[0]

    @pl.when(step == 0)
    def _():
        state_ref[...] = jnp.zeros_like(state_ref)
        keep_dev_ref = state_ref.at[heads * size :, :]
        write_factors(
            heads, docs, count, rate_ref, len_ref, first_ref, factor_ref, keep_ref, keep_dev_ref, covered_ref
        )

    at_rows = pl.ds(pl.multiple_of(step * rows, rows), rows)
    for h in range(heads):
        at = head_cols(h, size)
        leave = factor_ref[LEAVE_DEV * heads + h : LEAVE_DEV * heads + h + 1, at_rows]
        state_ref[state_rows(h, size), :] += dot_nn(scaled_half(key_ref[:, at].T, leave), value_ref[:, at])


def local_states(keys, values, rates, lengths, first, count, heads, size):
    rows, width = keys.shape
    docs = lengths.shape[0]
    step_rows = min(ROWS_AND_VMEM["local_state"][0], rows)
    blocks = rows // BLOCK
    shapes = (packed_shape(heads, size), (LANES, rows), (blocks, 3 * heads, LANES))
    smem = pl.BlockSpec(memory_space=pltpu.SMEM)
    return pl.pallas_call(
        functools.partial(state_kernel, heads, size, docs, count),
        grid=(rows // step_rows,),
        in_specs=[
            smem,
            smem,
            whole_spec((heads, rows)),
            spec((step_rows, width), lambda i: (i, 0)),
            spec((step_rows, width), lambda i: (i, 0)),
        ],
        out_specs=[whole_spec(s) for s in shapes] + [smem],
        out_shape=[jax.ShapeDtypeStruct(s, F32) for s in shapes] + [jax.ShapeDtypeStruct((2,), jnp.int32)],
        compiler_params=params("local_state"),
        cost_estimate=cost(2 * rows * width * size, 4 * rows * width),
        name="local_state",
    )(lengths, first, rates, keys, values)


def column(col, group, heads, h):
    return col[:, group * heads + h : group * heads + h + 1]


def block_weights(heads, col, factor_ref, h, bias):
    return jnp.exp(column(col, RUN, heads, h) - factor_ref[RUN * heads + h : RUN * heads + h + 1, :] + bias)


def block_bias(heads, col, factor_ref):
    causal = lax.broadcasted_iota(jnp.int32, (BLOCK, BLOCK), 0) >= lax.broadcasted_iota(
        jnp.int32, (BLOCK, BLOCK), 1
    )
    same = column(col, DOC, heads, 0) == factor_ref[DOC * heads : DOC * heads + 1, :]
    return jnp.where(causal & same, 0.0, -1e30)


def keep_row(keep_ref, group, heads, h):
    return keep_ref[0, group * heads + h : group * heads + h + 1, :]


def forward_kernel(
    heads, size, query_ref, key_ref, value_ref, factor_ref, keep_ref,
    raw_ref, probs_ref, states_ref, query_out_ref, key_out_ref, value_out_ref, state_ref,
):
    step = pl.program_id(0)

    @pl.when(step == 0)
    def _():
        state_ref[...] = jnp.zeros_like(state_ref)

    col = factor_ref[...].T
    bias = block_bias(heads, col, factor_ref)
    for h in range(heads):
        at = head_cols(h, size)
        query, key, value = query_ref[:, at], key_ref[:, at], value_ref[:, at]
        leave = column(col, LEAVE, heads, h)
        keep_from = keep_row(keep_ref, KEEP_FROM, heads, h)
        weights = block_weights(heads, col, factor_ref, h, bias)
        probs = (dot_nt(query, key) * weights).astype(BF16)
        state = state_ref[h]
        state_half = state.astype(BF16)
        probs_ref[0, h] = probs
        states_ref[0, h] = state_half
        entered = query.astype(F32) * column(col, ENTER, heads, h)
        left = key.astype(F32) * leave
        query_out_ref[:, at] = (entered * keep_row(keep_ref, KEEP_TO, heads, h)).astype(BF16)
        key_out_ref[:, at] = (left * keep_from).astype(BF16)
        value_out_ref[:, at] = (value.astype(F32) * leave * keep_from).astype(BF16)
        both = jnp.concatenate([probs, entered.astype(BF16)], axis=1)
        raw = dot_nn(both, jnp.concatenate([value, state_half], axis=0))
        raw_ref[:, at] = raw.astype(BF16)
        state_ref[h] = keep_row(keep_ref, KEEP, heads, h) * state + dot_tn(left.astype(BF16), value)


def forward_local(queries, keys, values, factors, keep, heads, size):
    rows, width = queries.shape
    blocks = rows // BLOCK
    token = spec((BLOCK, width), lambda i: (i, 0))
    per_block = spec((1, heads, size, size), lambda i: (i, 0, 0, 0))
    token_shape = jax.ShapeDtypeStruct((rows, width), BF16)
    return pl.pallas_call(
        functools.partial(forward_kernel, heads, size),
        grid=(blocks,),
        in_specs=[
            token,
            token,
            token,
            spec((LANES, BLOCK), lambda i: (0, i)),
            spec((1,) + keep.shape[1:], lambda i: (i, 0, 0)),
        ],
        out_specs=[token, per_block, per_block, token, token, token],
        out_shape=[
            token_shape,
            jax.ShapeDtypeStruct((blocks, heads, BLOCK, BLOCK), BF16),
            jax.ShapeDtypeStruct((blocks, heads, size, size), BF16),
            token_shape,
            token_shape,
            token_shape,
        ],
        scratch_shapes=[pltpu.VMEM((heads, size, size), F32)],
        compiler_params=params("forward_local"),
        cost_estimate=cost(8 * rows * width * size, 18 * rows * width),
        name="forward_local",
    )(queries, keys, values, factors, keep)


def state_rows(h, size):
    return slice(h * size, (h + 1) * size)


def entering_state(received, heads, size, h):
    keep_at = slice(heads * size + h, heads * size + h + 1)
    total = received[-1][state_rows(h, size), :]
    for packed in reversed(received[:-1]):
        total = packed[state_rows(h, size), :] + packed[keep_at, :] * total
    return total


def packed_shape(heads, size):
    return (heads * size + heads, LANES)


def raw_kernel(heads, size, hops, raw_ref, query_ref, grad_ref, gain_ref, *rest):
    received = rest[:hops]
    out_ref, sums_ref, enter_ref = rest[hops:]
    step = pl.program_id(0)
    rows = raw_ref.shape[0]

    @pl.when(step == 0)
    def _():
        for h in range(heads):
            enter_ref[h] = entering_state(received, heads, size, h).astype(BF16)

    squares = jnp.zeros((rows, size), F32)
    projected = jnp.zeros((rows, size), F32)
    for h in range(heads):
        at = head_cols(h, size)
        raw = raw_ref[:, at].astype(F32) + dot_nn(query_ref[:, at], enter_ref[h])
        out_ref[:, at] = raw.astype(BF16)
        squares = squares + raw * raw
        projected = projected + grad_ref[:, at].astype(F32) * gain_ref[:, at] * raw
    lane = lax.broadcasted_iota(jnp.int32, (rows, LANES), 1)
    packed = jnp.where(
        lane == 0,
        jnp.sum(squares, axis=1, keepdims=True),
        jnp.where(lane == 1, jnp.sum(projected, axis=1, keepdims=True), 0.0),
    )
    sums_ref[...] = packed.T[0:8, :]


def raw_and_sums(raw, queries, out_grad, gain, received, heads, size):
    rows, width = queries.shape
    step_rows = min(ROWS_AND_VMEM["raw_and_sums"][0], rows)
    token = spec((step_rows, width), lambda i: (i, 0))
    state_shape = (heads, size, size)
    return pl.pallas_call(
        functools.partial(raw_kernel, heads, size, len(received)),
        grid=(rows // step_rows,),
        in_specs=[
            token,
            token,
            token,
            whole_spec((1, width)),
        ]
        + [whole_spec(packed_shape(heads, size))] * len(received),
        out_specs=[token, spec((8, step_rows), lambda i: (0, i)), whole_spec(state_shape)],
        out_shape=[
            jax.ShapeDtypeStruct((rows, width), BF16),
            jax.ShapeDtypeStruct((8, rows), F32),
            jax.ShapeDtypeStruct(state_shape, BF16),
        ],
        compiler_params=params("raw_and_sums"),
        cost_estimate=cost(2 * rows * width * size, 8 * rows * width),
        name="raw_and_sums",
    )(raw, queries, out_grad, gain, *received)


def carry_kernel(heads, size, full_width, parts, raw_ref, query_ref, grad_ref, gain_ref, state_in_ref, *rest):
    sums = rest[:parts]
    carry_ref, scale_ref = rest[parts:]
    step = pl.program_id(0)
    rows = raw_ref.shape[0]

    @pl.when(step == 0)
    def _():
        carry_ref[...] = jnp.zeros_like(carry_ref)
        carry_ref[heads * size :, :] = state_in_ref[...]

    total = sums[0][...]
    for part in sums[1:]:
        total = total + part[...]
    total = jnp.concatenate([total, jnp.zeros((LANES - 8, rows), F32)], axis=0).T
    inverse = lax.rsqrt(total[:, 0:1] / full_width + EPS)
    slope = inverse * inverse * inverse * total[:, 1:2] / full_width
    lane = lax.broadcasted_iota(jnp.int32, (rows, LANES), 1)
    scale_ref[...] = jnp.where(lane == 0, inverse, slope)
    for h in range(heads):
        at = head_cols(h, size)
        scaled = grad_ref[:, at].astype(F32) * gain_ref[:, at]
        grad_raw = (inverse * scaled - raw_ref[:, at].astype(F32) * slope).astype(BF16)
        carry_ref[state_rows(h, size), :] += dot_tn(query_ref[:, at], grad_raw)


def carry_states(raw, queries, out_grad, gain, state, sums, full_width, heads, size):
    rows, width = queries.shape
    step_rows = min(ROWS_AND_VMEM["carry_state"][0], rows)
    token = spec((step_rows, width), lambda i: (i, 0))
    narrow = spec((step_rows, LANES), lambda i: (i, 0))
    packed = packed_shape(heads, size)
    return pl.pallas_call(
        functools.partial(carry_kernel, heads, size, full_width, len(sums)),
        grid=(rows // step_rows,),
        in_specs=[token, token, token, whole_spec((1, width)), spec((heads, LANES), lambda i: (size, 0))]
        + [spec((8, step_rows), lambda i: (0, i))] * len(sums),
        out_specs=[whole_spec(packed), narrow],
        out_shape=[
            jax.ShapeDtypeStruct(packed, F32),
            jax.ShapeDtypeStruct((rows, LANES), F32),
        ],
        compiler_params=params("carry_state"),
        cost_estimate=cost(2 * rows * width * size, 6 * rows * width),
        name="carry_state",
    )(raw, queries, out_grad, gain, state, *sums)


def backward_kernel(
    heads, size, query_ref, key_ref, value_ref, raw_ref, out_grad_ref, gain_ref, scale_ref,
    factor_ref, keep_ref, probs_ref, states_ref, enter_ref,
    normed_ref, grad_query_ref, grad_key_ref, grad_value_ref, carry_ref,
):
    step = pl.program_id(0)

    @pl.when(step == 0)
    def _():
        carry_ref[...] = jnp.zeros_like(carry_ref)

    col = factor_ref[...].T
    bias = block_bias(heads, col, factor_ref)
    inverse, slope = scale_ref[:, 0:1], scale_ref[:, 1:2]
    for h in range(heads):
        at = head_cols(h, size)
        query, key, value = query_ref[:, at], key_ref[:, at], value_ref[:, at]
        raw, gain = raw_ref[:, at].astype(F32), gain_ref[:, at]
        enter, leave = column(col, ENTER, heads, h), column(col, LEAVE, heads, h)
        grad_raw = (inverse * (out_grad_ref[:, at].astype(F32) * gain) - raw * slope).astype(BF16)
        normed_ref[:, at] = (raw * inverse * gain).astype(BF16)
        weights = block_weights(heads, col, factor_ref, h, bias)
        mixed = (dot_nt(grad_raw, value) * weights).astype(BF16)
        prefix = keep_row(keep_ref, KEEP_TO, heads, h)
        state = (states_ref[0, h].astype(F32) + prefix * enter_ref[h].astype(F32)).astype(BF16)
        grad_query = dot_nn(mixed, key) + enter * dot_nt(grad_raw, state)
        grad_query_ref[:, at] = grad_query.astype(BF16)
        carry = carry_ref[h]
        carry_half = carry.astype(BF16)
        grad_key = dot_tn(mixed, query) + leave * dot_nt(value, carry_half)
        grad_value = dot_tn(probs_ref[0, h], grad_raw) + leave * dot_nn(key, carry_half)
        grad_key_ref[:, at] = grad_key.astype(BF16)
        grad_value_ref[:, at] = grad_value.astype(BF16)
        enter_row = factor_ref[ENTER * heads + h : ENTER * heads + h + 1, :]
        update = dot_nn(scaled_half(query.T, enter_row), grad_raw)
        carry_ref[h] = keep_row(keep_ref, KEEP, heads, h) * carry + update


def backward_local(
    queries, keys, values, raw, out_grad, gain, scale, factors, keep, probs, states, entering, heads, size
):
    rows, width = queries.shape
    blocks = rows // BLOCK
    token = spec((BLOCK, width), lambda i: (blocks - 1 - i, 0))
    narrow = spec((BLOCK, LANES), lambda i: (blocks - 1 - i, 0))
    per_block = spec((1, heads, size, size), lambda i: (blocks - 1 - i, 0, 0, 0))
    return pl.pallas_call(
        functools.partial(backward_kernel, heads, size),
        grid=(blocks,),
        in_specs=[
            token,
            token,
            token,
            token,
            token,
            whole_spec((1, width)),
            narrow,
            spec((LANES, BLOCK), lambda i: (0, blocks - 1 - i)),
            spec((1,) + keep.shape[1:], lambda i: (blocks - 1 - i, 0, 0)),
            per_block,
            per_block,
            whole_spec((heads, size, size)),
        ],
        out_specs=[token] * 4,
        out_shape=[jax.ShapeDtypeStruct((rows, width), BF16)] * 4,
        scratch_shapes=[pltpu.VMEM((heads, size, size), F32)],
        compiler_params=params("backward_local"),
        cost_estimate=cost(16 * rows * width * size, 22 * rows * width),
        name="backward_local",
    )(queries, keys, values, raw, out_grad, gain, scale, factors, keep, probs, states, entering)


def finish_kernel(heads, size, hops, key_ref, value_ref, grad_key_ref, grad_value_ref, *rest):
    received = rest[:hops]
    key_out_ref, value_out_ref, beyond_ref = rest[hops:]
    step = pl.program_id(0)

    @pl.when(step == 0)
    def _():
        for h in range(heads):
            beyond_ref[h] = entering_state(received, heads, size, h).astype(BF16)

    for h in range(heads):
        at = head_cols(h, size)
        beyond = beyond_ref[h]
        grad_key = grad_key_ref[:, at].astype(F32) + dot_nt(value_ref[:, at], beyond)
        grad_value = grad_value_ref[:, at].astype(F32) + dot_nn(key_ref[:, at], beyond)
        key_out_ref[:, at] = grad_key.astype(BF16)
        value_out_ref[:, at] = grad_value.astype(BF16)


def finish(keys, values, grad_key, grad_value, received, heads, size):
    rows, width = keys.shape
    step_rows = min(ROWS_AND_VMEM["finish"][0], rows)
    token = spec((step_rows, width), lambda i: (i, 0))
    return pl.pallas_call(
        functools.partial(finish_kernel, heads, size, len(received)),
        grid=(rows // step_rows,),
        in_specs=[token] * 4
        + [whole_spec(packed_shape(heads, size))] * len(received),
        out_specs=[token, token],
        out_shape=[jax.ShapeDtypeStruct((rows, width), BF16)] * 2,
        scratch_shapes=[pltpu.VMEM((heads, size, size), BF16)],
        compiler_params=params("finish"),
        cost_estimate=cost(4 * rows * width * size, 12 * rows * width),
        name="finish",
    )(keys, values, grad_key, grad_value, *received)


def send_on(value, count, hops, towards, senders):
    received = []
    for j in range(1, hops + 1):
        ahead = towards * j
        pairs = [(i, i + ahead) for i in range(count) if 0 <= i + ahead < count and (j == 1 or i in senders[j])]
        received.append(lax.ppermute(value, "seq", pairs) if pairs else jnp.zeros_like(value))
    return received


def exchange(value, count, hops, towards, parity, crowded, local):
    everyone = {j: range(count) for j in range(2, hops + 1)}
    some = {j: range(parity, count, 2) if j == 2 else () for j in range(2, hops + 1)}

    def branch(senders):
        def run(value):
            received = send_on(value, count, hops, towards, senders)
            return received, local()

        return run

    if hops == 1:
        return branch({})(value)
    return lax.switch(crowded, [branch(some), branch(everyone)], value)


def body(queries, keys, values, log_decay, gain, lengths, out_grad):
    rows, heads = log_decay.shape
    width = queries.shape[1]
    size = width // heads
    count = lax.axis_size("seq")
    groups = lax.axis_size("head")
    full_width = width * groups
    longest = rows * count // DOC_SHARE
    hops = max(1, min(count - 1, -(-(longest - 1) // rows)))
    first = (lax.axis_index("seq") * rows).astype(jnp.int32).reshape(1)
    gain = gain.reshape(1, width)

    state, factors, keep, covered = local_states(
        keys, values, log_decay.T, lengths, first, count, heads, size
    )
    before, (raw, probs, states, query_in, key_out, value_out) = exchange(
        state, count, hops, 1, 0, covered[0],
        lambda: forward_local(queries, keys, values, factors, keep, heads, size),
    )
    raw, sums, entering = raw_and_sums(raw, query_in, out_grad, gain, before, heads, size)
    every = [sums] + [
        lax.ppermute(sums, "head", [(i, (i + j) % groups) for i in range(groups)]) for j in range(1, groups)
    ]
    carry, scale = carry_states(raw, query_in, out_grad, gain, state, every, full_width, heads, size)
    after, (normed, grad_query, grad_key, grad_value) = exchange(
        carry, count, hops, -1, 1, covered[1],
        lambda: backward_local(
            queries, keys, values, raw, out_grad, gain, scale, factors, keep, probs, states, entering, heads, size
        ),
    )
    grad_key, grad_value = finish(key_out, value_out, grad_key, grad_value, after, heads, size)
    return (normed, grad_query, grad_key, grad_value)


def solution(mesh):
    token = P("seq", "head")
    in_specs = (token, token, token, token, P("head"), P(), token)
    return jax.shard_map(body, mesh=mesh, in_specs=in_specs, out_specs=(token,) * 4, check_vma=False)
```

```python
import functools

import jax
import jax.numpy as jnp
from jax import lax
from jax.experimental import pallas as pl
from jax.experimental.pallas import tpu as pltpu
from jax.sharding import PartitionSpec as P

BLOCK = 128
LANES = 128
EPS = 1e-06
F32 = jnp.float32
BF16 = jnp.bfloat16
ROWS_AND_VMEM = {
    "local_state": (512, 58),
    "forward_local": (BLOCK, 14),
    "raw_and_sums": (512, 26),
    "carry_state": (512, 26),
    "backward_local": (BLOCK, 16),
    "finish": (512, 30),
}
DOC_SHARE = 4


def dot_nn(left, right):
    return lax.dot_general(left, right, (((1,), (0,)), ((), ())), preferred_element_type=F32)


def dot_nt(left, right):
    return lax.dot_general(left, right, (((1,), (1,)), ((), ())), preferred_element_type=F32)


def dot_tn(left, right):
    return lax.dot_general(left, right, (((0,), (0,)), ((), ())), preferred_element_type=F32)


def head_cols(index, size):
    return slice(index * size, (index + 1) * size)


def scaled_half(array, factor):
    return (array.astype(F32) * factor).astype(BF16)


def spec(shape, index_map):
    return pl.BlockSpec(shape, index_map)


def whole_spec(shape):
    rank = len(shape)
    return pl.BlockSpec(shape, lambda i: (0,) * rank)


def params(name):
    return pltpu.CompilerParams(vmem_limit_bytes=ROWS_AND_VMEM[name][1] * 1024 * 1024)


def cost(flops, bytes_accessed):
    return pl.CostEstimate(flops=flops, bytes_accessed=bytes_accessed, transcendentals=0)


RUN, ENTER, LEAVE, LEAVE_DEV, DOC = range(5)
KEEP, KEEP_TO, KEEP_FROM = range(3)


def count_docs(place, ends):
    total = jnp.zeros_like(place)
    for end in ends:
        total = total + (place >= end).astype(jnp.int32)
    return total


def write_covered(count, rows, ends, covered_ref):
    found = [0, 0]
    for i in range(count):
        at_edge = 0
        for end in ends:
            at_edge = at_edge + ((end >= i * rows) & (end <= (i + 1) * rows)).astype(jnp.int32)
        found[i % 2] = found[i % 2] + (at_edge == 0).astype(jnp.int32)
    for parity in range(2):
        covered_ref[parity] = jnp.minimum(found[parity], 1)


def write_factors(heads, docs, count, rate_ref, len_ref, first_ref, factor_ref, keep_ref, keep_dev_ref, covered_ref):
    rows = rate_ref.shape[1]
    blocks = rows // BLOCK
    first = first_ref[0]
    ends, total = [], 0
    for i in range(docs):
        total = total + len_ref[i]
        ends.append(total)
    write_covered(count, rows, ends, covered_ref)

    def doc_at(place):
        return jnp.where(place >= 0, count_docs(place, ends), -1)

    upper = (
        lax.broadcasted_iota(jnp.int32, (BLOCK, BLOCK), 0)
        <= lax.broadcasted_iota(jnp.int32, (BLOCK, BLOCK), 1)
    ).astype(F32)
    runs = [
        lax.dot_general(
            rate_ref[:, b * BLOCK : (b + 1) * BLOCK], upper, (((1,), (0,)), ((), ())),
            precision=lax.Precision.HIGHEST, preferred_element_type=F32,
        )
        for b in range(blocks)
    ]
    doc_before = doc_at(first - 1)
    doc_end = doc_at(first + rows - 1)
    filler = jnp.zeros((LANES - DOC * heads - 1, BLOCK), F32)
    keeps = []
    beyond = jnp.zeros((heads, 1), F32)
    for b in reversed(range(blocks)):
        at = slice(b * BLOCK, (b + 1) * BLOCK)
        start = first + b * BLOCK
        doc = count_docs(start + lax.broadcasted_iota(jnp.int32, (1, BLOCK), 1), ends)
        doc_start, doc_last = doc_at(start - 1), doc_at(start + BLOCK - 1)
        run = runs[b]
        last = run[:, BLOCK - 1 : BLOCK]
        factor_ref[RUN * heads : (RUN + 1) * heads, at] = run
        factor_ref[ENTER * heads : (ENTER + 1) * heads, at] = jnp.exp(run) * (doc == doc_start).astype(F32)
        factor_ref[LEAVE * heads : (LEAVE + 1) * heads, at] = jnp.exp(last - run) * (doc == doc_last).astype(F32)
        factor_ref[LEAVE_DEV * heads : (LEAVE_DEV + 1) * heads, at] = (
            jnp.exp(beyond + (last - run)) * (doc == doc_end).astype(F32)
        )
        factor_ref[DOC * heads : DOC * heads + 1, at] = doc.astype(F32)
        factor_ref[DOC * heads + 1 :, at] = filler
        beyond = beyond + last
        keeps.append(jnp.exp(jnp.broadcast_to(last, (heads, LANES))) * (doc_last == doc_start).astype(F32))
    keeps = keeps[::-1]
    to = jnp.ones((heads, LANES), F32)
    for b in range(blocks):
        keep_ref[b, KEEP * heads : (KEEP + 1) * heads, :] = keeps[b]
        keep_ref[b, KEEP_TO * heads : (KEEP_TO + 1) * heads, :] = to
        to = to * keeps[b]
    keep_dev_ref[...] = jnp.exp(jnp.broadcast_to(beyond, (heads, LANES))) * (doc_end == doc_before).astype(F32)
    after = jnp.ones((heads, LANES), F32)
    for b in reversed(range(blocks)):
        keep_ref[b, KEEP_FROM * heads : (KEEP_FROM + 1) * heads, :] = after
        after = after * keeps[b]


def state_kernel(
    heads, size, docs, count, len_ref, first_ref, rate_ref, key_ref, value_ref,
    state_ref, factor_ref, keep_ref, covered_ref,
):
    step = pl.program_id(0)
    rows = key_ref.shape[0]

    @pl.when(step == 0)
    def _():
        state_ref[...] = jnp.zeros_like(state_ref)
        keep_dev_ref = state_ref.at[heads * size :, :]
        write_factors(
            heads, docs, count, rate_ref, len_ref, first_ref, factor_ref, keep_ref, keep_dev_ref, covered_ref
        )

    at_rows = pl.ds(pl.multiple_of(step * rows, rows), rows)
    for h in range(heads):
        at = head_cols(h, size)
        leave = factor_ref[LEAVE_DEV * heads + h : LEAVE_DEV * heads + h + 1, at_rows]
        state_ref[state_rows(h, size), :] += dot_nn(scaled_half(key_ref[:, at].T, leave), value_ref[:, at])


def local_states(keys, values, rates, lengths, first, count, heads, size):
    rows, width = keys.shape
    docs = lengths.shape[0]
    step_rows = min(ROWS_AND_VMEM["local_state"][0], rows)
    blocks = rows // BLOCK
    shapes = (packed_shape(heads, size), (LANES, rows), (blocks, 3 * heads, LANES))
    smem = pl.BlockSpec(memory_space=pltpu.SMEM)
    return pl.pallas_call(
        functools.partial(state_kernel, heads, size, docs, count),
        grid=(rows // step_rows,),
        in_specs=[
            smem,
            smem,
            whole_spec((heads, rows)),
            spec((step_rows, width), lambda i: (i, 0)),
            spec((step_rows, width), lambda i: (i, 0)),
        ],
        out_specs=[whole_spec(s) for s in shapes] + [smem],
        out_shape=[jax.ShapeDtypeStruct(s, F32) for s in shapes] + [jax.ShapeDtypeStruct((2,), jnp.int32)],
        compiler_params=params("local_state"),
        cost_estimate=cost(2 * rows * width * size, 4 * rows * width),
        name="local_state",
    )(lengths, first, rates, keys, values)


def column(col, group, heads, h):
    return col[:, group * heads + h : group * heads + h + 1]


def block_weights(heads, col, factor_ref, h, bias):
    return jnp.exp(column(col, RUN, heads, h) - factor_ref[RUN * heads + h : RUN * heads + h + 1, :] + bias)


def block_bias(heads, col, factor_ref):
    causal = lax.broadcasted_iota(jnp.int32, (BLOCK, BLOCK), 0) >= lax.broadcasted_iota(
        jnp.int32, (BLOCK, BLOCK), 1
    )
    same = column(col, DOC, heads, 0) == factor_ref[DOC * heads : DOC * heads + 1, :]
    return jnp.where(causal & same, 0.0, -1e30)


def keep_row(keep_ref, group, heads, h):
    return keep_ref[0, group * heads + h : group * heads + h + 1, :]


def forward_kernel(
    heads, size, query_ref, key_ref, value_ref, factor_ref, keep_ref,
    raw_ref, probs_ref, states_ref, query_out_ref, key_out_ref, value_out_ref, state_ref,
):
    step = pl.program_id(0)

    @pl.when(step == 0)
    def _():
        state_ref[...] = jnp.zeros_like(state_ref)

    col = factor_ref[...].T
    bias = block_bias(heads, col, factor_ref)
    for h in range(heads):
        at = head_cols(h, size)
        query, key, value = query_ref[:, at], key_ref[:, at], value_ref[:, at]
        leave = column(col, LEAVE, heads, h)
        keep_from = keep_row(keep_ref, KEEP_FROM, heads, h)
        weights = block_weights(heads, col, factor_ref, h, bias)
        probs = (dot_nt(query, key) * weights).astype(BF16)
        state = state_ref[h]
        state_half = state.astype(BF16)
        probs_ref[0, h] = probs
        states_ref[0, h] = state_half
        entered = query.astype(F32) * column(col, ENTER, heads, h)
        left = key.astype(F32) * leave
        query_out_ref[:, at] = (entered * keep_row(keep_ref, KEEP_TO, heads, h)).astype(BF16)
        key_out_ref[:, at] = (left * keep_from).astype(BF16)
        value_out_ref[:, at] = (value.astype(F32) * leave * keep_from).astype(BF16)
        both = jnp.concatenate([probs, entered.astype(BF16)], axis=1)
        raw = dot_nn(both, jnp.concatenate([value, state_half], axis=0))
        raw_ref[:, at] = raw.astype(BF16)
        state_ref[h] = keep_row(keep_ref, KEEP, heads, h) * state + dot_tn(left.astype(BF16), value)


def forward_local(queries, keys, values, factors, keep, heads, size):
    rows, width = queries.shape
    blocks = rows // BLOCK
    token = spec((BLOCK, width), lambda i: (i, 0))
    per_block = spec((1, heads, size, size), lambda i: (i, 0, 0, 0))
    token_shape = jax.ShapeDtypeStruct((rows, width), BF16)
    return pl.pallas_call(
        functools.partial(forward_kernel, heads, size),
        grid=(blocks,),
        in_specs=[
            token,
            token,
            token,
            spec((LANES, BLOCK), lambda i: (0, i)),
            spec((1,) + keep.shape[1:], lambda i: (i, 0, 0)),
        ],
        out_specs=[token, per_block, per_block, token, token, token],
        out_shape=[
            token_shape,
            jax.ShapeDtypeStruct((blocks, heads, BLOCK, BLOCK), BF16),
            jax.ShapeDtypeStruct((blocks, heads, size, size), BF16),
            token_shape,
            token_shape,
            token_shape,
        ],
        scratch_shapes=[pltpu.VMEM((heads, size, size), F32)],
        compiler_params=params("forward_local"),
        cost_estimate=cost(8 * rows * width * size, 18 * rows * width),
        name="forward_local",
    )(queries, keys, values, factors, keep)


def state_rows(h, size):
    return slice(h * size, (h + 1) * size)


def entering_state(received, heads, size, h):
    keep_at = slice(heads * size + h, heads * size + h + 1)
    total = received[-1][state_rows(h, size), :]
    for packed in reversed(received[:-1]):
        total = packed[state_rows(h, size), :] + packed[keep_at, :] * total
    return total


def packed_shape(heads, size):
    return (heads * size + heads, LANES)


def raw_kernel(heads, size, hops, raw_ref, query_ref, grad_ref, gain_ref, *rest):
    received = rest[:hops]
    out_ref, sums_ref, enter_ref = rest[hops:]
    step = pl.program_id(0)
    rows = raw_ref.shape[0]

    @pl.when(step == 0)
    def _():
        for h in range(heads):
            enter_ref[h] = entering_state(received, heads, size, h).astype(BF16)

    squares = jnp.zeros((rows, size), F32)
    projected = jnp.zeros((rows, size), F32)
    for h in range(heads):
        at = head_cols(h, size)
        raw = raw_ref[:, at].astype(F32) + dot_nn(query_ref[:, at], enter_ref[h])
        out_ref[:, at] = raw.astype(BF16)
        squares = squares + raw * raw
        projected = projected + grad_ref[:, at].astype(F32) * gain_ref[:, at] * raw
    lane = lax.broadcasted_iota(jnp.int32, (rows, LANES), 1)
    packed = jnp.where(
        lane == 0,
        jnp.sum(squares, axis=1, keepdims=True),
        jnp.where(lane == 1, jnp.sum(projected, axis=1, keepdims=True), 0.0),
    )
    sums_ref[...] = packed.T[0:8, :]


def raw_and_sums(raw, queries, out_grad, gain, received, heads, size):
    rows, width = queries.shape
    step_rows = min(ROWS_AND_VMEM["raw_and_sums"][0], rows)
    token = spec((step_rows, width), lambda i: (i, 0))
    state_shape = (heads, size, size)
    return pl.pallas_call(
        functools.partial(raw_kernel, heads, size, len(received)),
        grid=(rows // step_rows,),
        in_specs=[
            token,
            token,
            token,
            whole_spec((1, width)),
        ]
        + [whole_spec(packed_shape(heads, size))] * len(received),
        out_specs=[token, spec((8, step_rows), lambda i: (0, i)), whole_spec(state_shape)],
        out_shape=[
            jax.ShapeDtypeStruct((rows, width), BF16),
            jax.ShapeDtypeStruct((8, rows), F32),
            jax.ShapeDtypeStruct(state_shape, BF16),
        ],
        compiler_params=params("raw_and_sums"),
        cost_estimate=cost(2 * rows * width * size, 8 * rows * width),
        name="raw_and_sums",
    )(raw, queries, out_grad, gain, *received)


def carry_kernel(heads, size, full_width, parts, raw_ref, query_ref, grad_ref, gain_ref, state_in_ref, *rest):
    sums = rest[:parts]
    carry_ref, scale_ref = rest[parts:]
    step = pl.program_id(0)
    rows = raw_ref.shape[0]

    @pl.when(step == 0)
    def _():
        carry_ref[...] = jnp.zeros_like(carry_ref)
        carry_ref[heads * size :, :] = state_in_ref[...]

    total = sums[0][...]
    for part in sums[1:]:
        total = total + part[...]
    total = jnp.concatenate([total, jnp.zeros((LANES - 8, rows), F32)], axis=0).T
    inverse = lax.rsqrt(total[:, 0:1] / full_width + EPS)
    slope = inverse * inverse * inverse * total[:, 1:2] / full_width
    lane = lax.broadcasted_iota(jnp.int32, (rows, LANES), 1)
    scale_ref[...] = jnp.where(lane == 0, inverse, slope)
    for h in range(heads):
        at = head_cols(h, size)
        scaled = grad_ref[:, at].astype(F32) * gain_ref[:, at]
        grad_raw = (inverse * scaled - raw_ref[:, at].astype(F32) * slope).astype(BF16)
        carry_ref[state_rows(h, size), :] += dot_tn(query_ref[:, at], grad_raw)


def carry_states(raw, queries, out_grad, gain, state, sums, full_width, heads, size):
    rows, width = queries.shape
    step_rows = min(ROWS_AND_VMEM["carry_state"][0], rows)
    token = spec((step_rows, width), lambda i: (i, 0))
    narrow = spec((step_rows, LANES), lambda i: (i, 0))
    packed = packed_shape(heads, size)
    return pl.pallas_call(
        functools.partial(carry_kernel, heads, size, full_width, len(sums)),
        grid=(rows // step_rows,),
        in_specs=[token, token, token, whole_spec((1, width)), spec((heads, LANES), lambda i: (size, 0))]
        + [spec((8, step_rows), lambda i: (0, i))] * len(sums),
        out_specs=[whole_spec(packed), narrow],
        out_shape=[
            jax.ShapeDtypeStruct(packed, F32),
            jax.ShapeDtypeStruct((rows, LANES), F32),
        ],
        compiler_params=params("carry_state"),
        cost_estimate=cost(2 * rows * width * size, 6 * rows * width),
        name="carry_state",
    )(raw, queries, out_grad, gain, state, *sums)


def backward_kernel(
    heads, size, query_ref, key_ref, value_ref, raw_ref, out_grad_ref, gain_ref, scale_ref,
    factor_ref, keep_ref, probs_ref, states_ref, enter_ref,
    normed_ref, grad_query_ref, grad_key_ref, grad_value_ref, carry_ref,
):
    step = pl.program_id(0)

    @pl.when(step == 0)
    def _():
        carry_ref[...] = jnp.zeros_like(carry_ref)

    col = factor_ref[...].T
    bias = block_bias(heads, col, factor_ref)
    inverse, slope = scale_ref[:, 0:1], scale_ref[:, 1:2]
    for h in range(heads):
        at = head_cols(h, size)
        query, key, value = query_ref[:, at], key_ref[:, at], value_ref[:, at]
        raw, gain = raw_ref[:, at].astype(F32), gain_ref[:, at]
        enter, leave = column(col, ENTER, heads, h), column(col, LEAVE, heads, h)
        grad_raw = (inverse * (out_grad_ref[:, at].astype(F32) * gain) - raw * slope).astype(BF16)
        normed_ref[:, at] = (raw * inverse * gain).astype(BF16)
        weights = block_weights(heads, col, factor_ref, h, bias)
        mixed = (dot_nt(grad_raw, value) * weights).astype(BF16)
        prefix = keep_row(keep_ref, KEEP_TO, heads, h)
        state = (states_ref[0, h].astype(F32) + prefix * enter_ref[h].astype(F32)).astype(BF16)
        grad_query = dot_nn(mixed, key) + enter * dot_nt(grad_raw, state)
        grad_query_ref[:, at] = grad_query.astype(BF16)
        carry = carry_ref[h]
        carry_half = carry.astype(BF16)
        grad_key = dot_tn(mixed, query) + leave * dot_nt(value, carry_half)
        grad_value = dot_tn(probs_ref[0, h], grad_raw) + leave * dot_nn(key, carry_half)
        grad_key_ref[:, at] = grad_key.astype(BF16)
        grad_value_ref[:, at] = grad_value.astype(BF16)
        update = dot_tn(scaled_half(query, enter), grad_raw)
        carry_ref[h] = keep_row(keep_ref, KEEP, heads, h) * carry + update


def backward_local(
    queries, keys, values, raw, out_grad, gain, scale, factors, keep, probs, states, entering, heads, size
):
    rows, width = queries.shape
    blocks = rows // BLOCK
    token = spec((BLOCK, width), lambda i: (blocks - 1 - i, 0))
    narrow = spec((BLOCK, LANES), lambda i: (blocks - 1 - i, 0))
    per_block = spec((1, heads, size, size), lambda i: (blocks - 1 - i, 0, 0, 0))
    return pl.pallas_call(
        functools.partial(backward_kernel, heads, size),
        grid=(blocks,),
        in_specs=[
            token,
            token,
            token,
            token,
            token,
            whole_spec((1, width)),
            narrow,
            spec((LANES, BLOCK), lambda i: (0, blocks - 1 - i)),
            spec((1,) + keep.shape[1:], lambda i: (blocks - 1 - i, 0, 0)),
            per_block,
            per_block,
            whole_spec((heads, size, size)),
        ],
        out_specs=[token] * 4,
        out_shape=[jax.ShapeDtypeStruct((rows, width), BF16)] * 4,
        scratch_shapes=[pltpu.VMEM((heads, size, size), F32)],
        compiler_params=params("backward_local"),
        cost_estimate=cost(16 * rows * width * size, 22 * rows * width),
        name="backward_local",
    )(queries, keys, values, raw, out_grad, gain, scale, factors, keep, probs, states, entering)


def finish_kernel(heads, size, hops, key_ref, value_ref, grad_key_ref, grad_value_ref, *rest):
    received = rest[:hops]
    key_out_ref, value_out_ref, beyond_ref = rest[hops:]
    step = pl.program_id(0)

    @pl.when(step == 0)
    def _():
        for h in range(heads):
            beyond_ref[h] = entering_state(received, heads, size, h).astype(BF16)

    for h in range(heads):
        at = head_cols(h, size)
        beyond = beyond_ref[h]
        grad_key = grad_key_ref[:, at].astype(F32) + dot_nt(value_ref[:, at], beyond)
        grad_value = grad_value_ref[:, at].astype(F32) + dot_nn(key_ref[:, at], beyond)
        key_out_ref[:, at] = grad_key.astype(BF16)
        value_out_ref[:, at] = grad_value.astype(BF16)


def finish(keys, values, grad_key, grad_value, received, heads, size):
    rows, width = keys.shape
    step_rows = min(ROWS_AND_VMEM["finish"][0], rows)
    token = spec((step_rows, width), lambda i: (i, 0))
    return pl.pallas_call(
        functools.partial(finish_kernel, heads, size, len(received)),
        grid=(rows // step_rows,),
        in_specs=[token] * 4
        + [whole_spec(packed_shape(heads, size))] * len(received),
        out_specs=[token, token],
        out_shape=[jax.ShapeDtypeStruct((rows, width), BF16)] * 2,
        scratch_shapes=[pltpu.VMEM((heads, size, size), BF16)],
        compiler_params=params("finish"),
        cost_estimate=cost(4 * rows * width * size, 12 * rows * width),
        name="finish",
    )(keys, values, grad_key, grad_value, *received)


def send_on(value, count, hops, towards, senders):
    received = []
    for j in range(1, hops + 1):
        ahead = towards * j
        pairs = [(i, i + ahead) for i in range(count) if 0 <= i + ahead < count and (j == 1 or i in senders[j])]
        received.append(lax.ppermute(value, "seq", pairs) if pairs else jnp.zeros_like(value))
    return received


def exchange(value, count, hops, towards, parity, crowded, local):
    everyone = {j: range(count) for j in range(2, hops + 1)}
    some = {j: range(parity, count, 2) if j == 2 else () for j in range(2, hops + 1)}

    def branch(senders):
        def run(value):
            received = send_on(value, count, hops, towards, senders)
            return received, local()

        return run

    if hops == 1:
        return branch({})(value)
    return lax.switch(crowded, [branch(some), branch(everyone)], value)


def body(queries, keys, values, log_decay, gain, lengths, out_grad):
    rows, heads = log_decay.shape
    width = queries.shape[1]
    size = width // heads
    count = lax.axis_size("seq")
    groups = lax.axis_size("head")
    full_width = width * groups
    longest = rows * count // DOC_SHARE
    hops = max(1, min(count - 1, -(-(longest - 1) // rows)))
    first = (lax.axis_index("seq") * rows).astype(jnp.int32).reshape(1)
    gain = gain.reshape(1, width)

    state, factors, keep, covered = local_states(
        keys, values, log_decay.T, lengths, first, count, heads, size
    )
    before, (raw, probs, states, query_in, key_out, value_out) = exchange(
        state, count, hops, 1, 0, covered[0],
        lambda: forward_local(queries, keys, values, factors, keep, heads, size),
    )
    raw, sums, entering = raw_and_sums(raw, query_in, out_grad, gain, before, heads, size)
    every = [sums] + [
        lax.ppermute(sums, "head", [(i, (i + j) % groups) for i in range(groups)]) for j in range(1, groups)
    ]
    carry, scale = carry_states(raw, query_in, out_grad, gain, state, every, full_width, heads, size)
    after, (normed, grad_query, grad_key, grad_value) = exchange(
        carry, count, hops, -1, 1, covered[1],
        lambda: backward_local(
            queries, keys, values, raw, out_grad, gain, scale, factors, keep, probs, states, entering, heads, size
        ),
    )
    grad_key, grad_value = finish(key_out, value_out, grad_key, grad_value, after, heads, size)
    return (normed, grad_query, grad_key, grad_value)


def solution(mesh):
    token = P("seq", "head")
    in_specs = (token, token, token, token, P("head"), P(), token)
    return jax.shard_map(body, mesh=mesh, in_specs=in_specs, out_specs=(token,) * 4, check_vma=False)
```

```python
import functools

import jax
import jax.numpy as jnp
from jax import lax
from jax.experimental import pallas as pl
from jax.experimental.pallas import tpu as pltpu
from jax.sharding import PartitionSpec as P

BLOCK = 128
LANES = 128
EPS = 1e-06
F32 = jnp.float32
BF16 = jnp.bfloat16
ROWS_AND_VMEM = {
    "local_state": (512, 58),
    "forward_local": (BLOCK, 14),
    "raw_and_sums": (512, 26),
    "carry_state": (512, 26),
    "backward_local": (BLOCK, 16),
    "finish": (512, 30),
}
DOC_SHARE = 4


def dot_nn(left, right):
    return lax.dot_general(left, right, (((1,), (0,)), ((), ())), preferred_element_type=F32)


def dot_nt(left, right):
    return lax.dot_general(left, right, (((1,), (1,)), ((), ())), preferred_element_type=F32)


def dot_tn(left, right):
    return lax.dot_general(left, right, (((0,), (0,)), ((), ())), preferred_element_type=F32)


def head_cols(index, size):
    return slice(index * size, (index + 1) * size)


def scaled_half(array, factor):
    return (array.astype(F32) * factor).astype(BF16)


def spec(shape, index_map):
    return pl.BlockSpec(shape, index_map)


def whole_spec(shape):
    rank = len(shape)
    return pl.BlockSpec(shape, lambda i: (0,) * rank)


def params(name):
    return pltpu.CompilerParams(vmem_limit_bytes=ROWS_AND_VMEM[name][1] * 1024 * 1024)


def cost(flops, bytes_accessed):
    return pl.CostEstimate(flops=flops, bytes_accessed=bytes_accessed, transcendentals=0)


RUN, ENTER, LEAVE, LEAVE_DEV, DOC = range(5)
KEEP, KEEP_TO, KEEP_FROM = range(3)


def count_docs(place, ends):
    total = jnp.zeros_like(place)
    for end in ends:
        total = total + (place >= end).astype(jnp.int32)
    return total


def write_covered(count, rows, ends, covered_ref):
    found = [0, 0]
    for i in range(count):
        at_edge = 0
        for end in ends:
            at_edge = at_edge + ((end >= i * rows) & (end <= (i + 1) * rows)).astype(jnp.int32)
        found[i % 2] = found[i % 2] + (at_edge == 0).astype(jnp.int32)
    for parity in range(2):
        covered_ref[parity][0] = jnp.minimum(found[parity], 1)


def write_factors(heads, docs, count, rate_ref, len_ref, first_ref, factor_ref, keep_ref, keep_dev_ref, covered_ref):
    rows = rate_ref.shape[1]
    blocks = rows // BLOCK
    first = first_ref[0]
    ends, total = [], 0
    for i in range(docs):
        total = total + len_ref[i]
        ends.append(total)
    write_covered(count, rows, ends, covered_ref)

    def doc_at(place):
        return jnp.where(place >= 0, count_docs(place, ends), -1)

    upper = (
        lax.broadcasted_iota(jnp.int32, (BLOCK, BLOCK), 0)
        <= lax.broadcasted_iota(jnp.int32, (BLOCK, BLOCK), 1)
    ).astype(F32)
    runs = [
        lax.dot_general(
            rate_ref[:, b * BLOCK : (b + 1) * BLOCK], upper, (((1,), (0,)), ((), ())),
            precision=lax.Precision.HIGHEST, preferred_element_type=F32,
        )
        for b in range(blocks)
    ]
    doc_before = doc_at(first - 1)
    doc_end = doc_at(first + rows - 1)
    filler = jnp.zeros((LANES - DOC * heads - 1, BLOCK), F32)
    keeps = []
    beyond = jnp.zeros((heads, 1), F32)
    for b in reversed(range(blocks)):
        at = slice(b * BLOCK, (b + 1) * BLOCK)
        start = first + b * BLOCK
        doc = count_docs(start + lax.broadcasted_iota(jnp.int32, (1, BLOCK), 1), ends)
        doc_start, doc_last = doc_at(start - 1), doc_at(start + BLOCK - 1)
        run = runs[b]
        last = run[:, BLOCK - 1 : BLOCK]
        factor_ref[RUN * heads : (RUN + 1) * heads, at] = run
        factor_ref[ENTER * heads : (ENTER + 1) * heads, at] = jnp.exp(run) * (doc == doc_start).astype(F32)
        factor_ref[LEAVE * heads : (LEAVE + 1) * heads, at] = jnp.exp(last - run) * (doc == doc_last).astype(F32)
        factor_ref[LEAVE_DEV * heads : (LEAVE_DEV + 1) * heads, at] = (
            jnp.exp(beyond + (last - run)) * (doc == doc_end).astype(F32)
        )
        factor_ref[DOC * heads : DOC * heads + 1, at] = doc.astype(F32)
        factor_ref[DOC * heads + 1 :, at] = filler
        beyond = beyond + last
        keeps.append(jnp.exp(jnp.broadcast_to(last, (heads, LANES))) * (doc_last == doc_start).astype(F32))
    keeps = keeps[::-1]
    to = jnp.ones((heads, LANES), F32)
    for b in range(blocks):
        keep_ref[b, KEEP * heads : (KEEP + 1) * heads, :] = keeps[b]
        keep_ref[b, KEEP_TO * heads : (KEEP_TO + 1) * heads, :] = to
        to = to * keeps[b]
    keep_dev_ref[...] = jnp.exp(jnp.broadcast_to(beyond, (heads, LANES))) * (doc_end == doc_before).astype(F32)
    after = jnp.ones((heads, LANES), F32)
    for b in reversed(range(blocks)):
        keep_ref[b, KEEP_FROM * heads : (KEEP_FROM + 1) * heads, :] = after
        after = after * keeps[b]


def state_kernel(
    heads, size, docs, count, len_ref, first_ref, rate_ref, key_ref, value_ref,
    state_ref, factor_ref, keep_ref, *covered_ref,
):
    step = pl.program_id(0)
    rows = key_ref.shape[0]

    @pl.when(step == 0)
    def _():
        state_ref[...] = jnp.zeros_like(state_ref)
        keep_dev_ref = state_ref.at[heads * size :, :]
        write_factors(
            heads, docs, count, rate_ref, len_ref, first_ref, factor_ref, keep_ref, keep_dev_ref, covered_ref
        )

    at_rows = pl.ds(pl.multiple_of(step * rows, rows), rows)
    for h in range(heads):
        at = head_cols(h, size)
        leave = factor_ref[LEAVE_DEV * heads + h : LEAVE_DEV * heads + h + 1, at_rows]
        state_ref[state_rows(h, size), :] += dot_nn(scaled_half(key_ref[:, at].T, leave), value_ref[:, at])


def local_states(keys, values, rates, lengths, first, count, heads, size):
    rows, width = keys.shape
    docs = lengths.shape[0]
    step_rows = min(ROWS_AND_VMEM["local_state"][0], rows)
    blocks = rows // BLOCK
    shapes = (packed_shape(heads, size), (LANES, rows), (blocks, 3 * heads, LANES))
    smem = pl.BlockSpec(memory_space=pltpu.SMEM)
    return pl.pallas_call(
        functools.partial(state_kernel, heads, size, docs, count),
        grid=(rows // step_rows,),
        in_specs=[
            smem,
            smem,
            whole_spec((heads, rows)),
            spec((step_rows, width), lambda i: (i, 0)),
            spec((step_rows, width), lambda i: (i, 0)),
        ],
        out_specs=[whole_spec(s) for s in shapes] + [smem] * 2,
        out_shape=[jax.ShapeDtypeStruct(s, F32) for s in shapes] + [jax.ShapeDtypeStruct((1,), jnp.int32)] * 2,
        compiler_params=params("local_state"),
        cost_estimate=cost(2 * rows * width * size, 4 * rows * width),
        name="local_state",
    )(lengths, first, rates, keys, values)


def column(col, group, heads, h):
    return col[:, group * heads + h : group * heads + h + 1]


def block_weights(heads, col, factor_ref, h, bias):
    return jnp.exp(column(col, RUN, heads, h) - factor_ref[RUN * heads + h : RUN * heads + h + 1, :] + bias)


def block_bias(heads, col, factor_ref):
    causal = lax.broadcasted_iota(jnp.int32, (BLOCK, BLOCK), 0) >= lax.broadcasted_iota(
        jnp.int32, (BLOCK, BLOCK), 1
    )
    same = column(col, DOC, heads, 0) == factor_ref[DOC * heads : DOC * heads + 1, :]
    return jnp.where(causal & same, 0.0, -1e30)


def keep_row(keep_ref, group, heads, h):
    return keep_ref[0, group * heads + h : group * heads + h + 1, :]


def forward_kernel(
    heads, size, query_ref, key_ref, value_ref, factor_ref, keep_ref,
    raw_ref, probs_ref, states_ref, query_out_ref, key_out_ref, value_out_ref, state_ref,
):
    step = pl.program_id(0)

    @pl.when(step == 0)
    def _():
        state_ref[...] = jnp.zeros_like(state_ref)

    col = factor_ref[...].T
    bias = block_bias(heads, col, factor_ref)
    for h in range(heads):
        at = head_cols(h, size)
        query, key, value = query_ref[:, at], key_ref[:, at], value_ref[:, at]
        leave = column(col, LEAVE, heads, h)
        keep_from = keep_row(keep_ref, KEEP_FROM, heads, h)
        weights = block_weights(heads, col, factor_ref, h, bias)
        probs = (dot_nt(query, key) * weights).astype(BF16)
        state = state_ref[h]
        state_half = state.astype(BF16)
        probs_ref[0, h] = probs
        states_ref[0, h] = state_half
        entered = query.astype(F32) * column(col, ENTER, heads, h)
        left = key.astype(F32) * leave
        query_out_ref[:, at] = (entered * keep_row(keep_ref, KEEP_TO, heads, h)).astype(BF16)
        key_out_ref[:, at] = (left * keep_from).astype(BF16)
        value_out_ref[:, at] = (value.astype(F32) * leave * keep_from).astype(BF16)
        both = jnp.concatenate([probs, entered.astype(BF16)], axis=1)
        raw = dot_nn(both, jnp.concatenate([value, state_half], axis=0))
        raw_ref[:, at] = raw.astype(BF16)
        state_ref[h] = keep_row(keep_ref, KEEP, heads, h) * state + dot_tn(left.astype(BF16), value)


def forward_local(queries, keys, values, factors, keep, heads, size):
    rows, width = queries.shape
    blocks = rows // BLOCK
    token = spec((BLOCK, width), lambda i: (i, 0))
    per_block = spec((1, heads, size, size), lambda i: (i, 0, 0, 0))
    token_shape = jax.ShapeDtypeStruct((rows, width), BF16)
    return pl.pallas_call(
        functools.partial(forward_kernel, heads, size),
        grid=(blocks,),
        in_specs=[
            token,
            token,
            token,
            spec((LANES, BLOCK), lambda i: (0, i)),
            spec((1,) + keep.shape[1:], lambda i: (i, 0, 0)),
        ],
        out_specs=[token, per_block, per_block, token, token, token],
        out_shape=[
            token_shape,
            jax.ShapeDtypeStruct((blocks, heads, BLOCK, BLOCK), BF16),
            jax.ShapeDtypeStruct((blocks, heads, size, size), BF16),
            token_shape,
            token_shape,
            token_shape,
        ],
        scratch_shapes=[pltpu.VMEM((heads, size, size), F32)],
        compiler_params=params("forward_local"),
        cost_estimate=cost(8 * rows * width * size, 18 * rows * width),
        name="forward_local",
    )(queries, keys, values, factors, keep)


def state_rows(h, size):
    return slice(h * size, (h + 1) * size)


def entering_state(received, heads, size, h):
    keep_at = slice(heads * size + h, heads * size + h + 1)
    total = received[-1][state_rows(h, size), :]
    for packed in reversed(received[:-1]):
        total = packed[state_rows(h, size), :] + packed[keep_at, :] * total
    return total


def packed_shape(heads, size):
    return (heads * size + heads, LANES)


def raw_kernel(heads, size, hops, raw_ref, query_ref, grad_ref, gain_ref, *rest):
    received = rest[:hops]
    out_ref, sums_ref, enter_ref = rest[hops:]
    step = pl.program_id(0)
    rows = raw_ref.shape[0]

    @pl.when(step == 0)
    def _():
        for h in range(heads):
            enter_ref[h] = entering_state(received, heads, size, h).astype(BF16)

    squares = jnp.zeros((rows, size), F32)
    projected = jnp.zeros((rows, size), F32)
    for h in range(heads):
        at = head_cols(h, size)
        raw = raw_ref[:, at].astype(F32) + dot_nn(query_ref[:, at], enter_ref[h])
        out_ref[:, at] = raw.astype(BF16)
        squares = squares + raw * raw
        projected = projected + grad_ref[:, at].astype(F32) * gain_ref[:, at] * raw
    lane = lax.broadcasted_iota(jnp.int32, (rows, LANES), 1)
    packed = jnp.where(
        lane == 0,
        jnp.sum(squares, axis=1, keepdims=True),
        jnp.where(lane == 1, jnp.sum(projected, axis=1, keepdims=True), 0.0),
    )
    sums_ref[...] = packed.T[0:8, :]


def raw_and_sums(raw, queries, out_grad, gain, received, heads, size):
    rows, width = queries.shape
    step_rows = min(ROWS_AND_VMEM["raw_and_sums"][0], rows)
    token = spec((step_rows, width), lambda i: (i, 0))
    state_shape = (heads, size, size)
    return pl.pallas_call(
        functools.partial(raw_kernel, heads, size, len(received)),
        grid=(rows // step_rows,),
        in_specs=[
            token,
            token,
            token,
            whole_spec((1, width)),
        ]
        + [whole_spec(packed_shape(heads, size))] * len(received),
        out_specs=[token, spec((8, step_rows), lambda i: (0, i)), whole_spec(state_shape)],
        out_shape=[
            jax.ShapeDtypeStruct((rows, width), BF16),
            jax.ShapeDtypeStruct((8, rows), F32),
            jax.ShapeDtypeStruct(state_shape, BF16),
        ],
        compiler_params=params("raw_and_sums"),
        cost_estimate=cost(2 * rows * width * size, 8 * rows * width),
        name="raw_and_sums",
    )(raw, queries, out_grad, gain, *received)


def carry_kernel(heads, size, full_width, parts, raw_ref, query_ref, grad_ref, gain_ref, state_in_ref, *rest):
    sums = rest[:parts]
    carry_ref, scale_ref = rest[parts:]
    step = pl.program_id(0)
    rows = raw_ref.shape[0]

    @pl.when(step == 0)
    def _():
        carry_ref[...] = jnp.zeros_like(carry_ref)
        carry_ref[heads * size :, :] = state_in_ref[...]

    total = sums[0][...]
    for part in sums[1:]:
        total = total + part[...]
    total = jnp.concatenate([total, jnp.zeros((LANES - 8, rows), F32)], axis=0).T
    inverse = lax.rsqrt(total[:, 0:1] / full_width + EPS)
    slope = inverse * inverse * inverse * total[:, 1:2] / full_width
    lane = lax.broadcasted_iota(jnp.int32, (rows, LANES), 1)
    scale_ref[...] = jnp.where(lane == 0, inverse, slope)
    for h in range(heads):
        at = head_cols(h, size)
        scaled = grad_ref[:, at].astype(F32) * gain_ref[:, at]
        grad_raw = (inverse * scaled - raw_ref[:, at].astype(F32) * slope).astype(BF16)
        carry_ref[state_rows(h, size), :] += dot_tn(query_ref[:, at], grad_raw)


def carry_states(raw, queries, out_grad, gain, state, sums, full_width, heads, size):
    rows, width = queries.shape
    step_rows = min(ROWS_AND_VMEM["carry_state"][0], rows)
    token = spec((step_rows, width), lambda i: (i, 0))
    narrow = spec((step_rows, LANES), lambda i: (i, 0))
    packed = packed_shape(heads, size)
    return pl.pallas_call(
        functools.partial(carry_kernel, heads, size, full_width, len(sums)),
        grid=(rows // step_rows,),
        in_specs=[token, token, token, whole_spec((1, width)), spec((heads, LANES), lambda i: (size, 0))]
        + [spec((8, step_rows), lambda i: (0, i))] * len(sums),
        out_specs=[whole_spec(packed), narrow],
        out_shape=[
            jax.ShapeDtypeStruct(packed, F32),
            jax.ShapeDtypeStruct((rows, LANES), F32),
        ],
        compiler_params=params("carry_state"),
        cost_estimate=cost(2 * rows * width * size, 6 * rows * width),
        name="carry_state",
    )(raw, queries, out_grad, gain, state, *sums)


def backward_kernel(
    heads, size, query_ref, key_ref, value_ref, raw_ref, out_grad_ref, gain_ref, scale_ref,
    factor_ref, keep_ref, probs_ref, states_ref, enter_ref,
    normed_ref, grad_query_ref, grad_key_ref, grad_value_ref, carry_ref,
):
    step = pl.program_id(0)

    @pl.when(step == 0)
    def _():
        carry_ref[...] = jnp.zeros_like(carry_ref)

    col = factor_ref[...].T
    bias = block_bias(heads, col, factor_ref)
    inverse, slope = scale_ref[:, 0:1], scale_ref[:, 1:2]
    for h in range(heads):
        at = head_cols(h, size)
        query, key, value = query_ref[:, at], key_ref[:, at], value_ref[:, at]
        raw, gain = raw_ref[:, at].astype(F32), gain_ref[:, at]
        enter, leave = column(col, ENTER, heads, h), column(col, LEAVE, heads, h)
        grad_raw = (inverse * (out_grad_ref[:, at].astype(F32) * gain) - raw * slope).astype(BF16)
        normed_ref[:, at] = (raw * inverse * gain).astype(BF16)
        weights = block_weights(heads, col, factor_ref, h, bias)
        mixed = (dot_nt(grad_raw, value) * weights).astype(BF16)
        prefix = keep_row(keep_ref, KEEP_TO, heads, h)
        state = (states_ref[0, h].astype(F32) + prefix * enter_ref[h].astype(F32)).astype(BF16)
        grad_query = dot_nn(mixed, key) + enter * dot_nt(grad_raw, state)
        grad_query_ref[:, at] = grad_query.astype(BF16)
        carry = carry_ref[h]
        carry_half = carry.astype(BF16)
        grad_key = dot_tn(mixed, query) + leave * dot_nt(value, carry_half)
        grad_value = dot_tn(probs_ref[0, h], grad_raw) + leave * dot_nn(key, carry_half)
        grad_key_ref[:, at] = grad_key.astype(BF16)
        grad_value_ref[:, at] = grad_value.astype(BF16)
        update = dot_tn(scaled_half(query, enter), grad_raw)
        carry_ref[h] = keep_row(keep_ref, KEEP, heads, h) * carry + update


def backward_local(
    queries, keys, values, raw, out_grad, gain, scale, factors, keep, probs, states, entering, heads, size
):
    rows, width = queries.shape
    blocks = rows // BLOCK
    token = spec((BLOCK, width), lambda i: (blocks - 1 - i, 0))
    narrow = spec((BLOCK, LANES), lambda i: (blocks - 1 - i, 0))
    per_block = spec((1, heads, size, size), lambda i: (blocks - 1 - i, 0, 0, 0))
    return pl.pallas_call(
        functools.partial(backward_kernel, heads, size),
        grid=(blocks,),
        in_specs=[
            token,
            token,
            token,
            token,
            token,
            whole_spec((1, width)),
            narrow,
            spec((LANES, BLOCK), lambda i: (0, blocks - 1 - i)),
            spec((1,) + keep.shape[1:], lambda i: (blocks - 1 - i, 0, 0)),
            per_block,
            per_block,
            whole_spec((heads, size, size)),
        ],
        out_specs=[token] * 4,
        out_shape=[jax.ShapeDtypeStruct((rows, width), BF16)] * 4,
        scratch_shapes=[pltpu.VMEM((heads, size, size), F32)],
        compiler_params=params("backward_local"),
        cost_estimate=cost(16 * rows * width * size, 22 * rows * width),
        name="backward_local",
    )(queries, keys, values, raw, out_grad, gain, scale, factors, keep, probs, states, entering)


def finish_kernel(heads, size, hops, key_ref, value_ref, grad_key_ref, grad_value_ref, *rest):
    received = rest[:hops]
    key_out_ref, value_out_ref, beyond_ref = rest[hops:]
    step = pl.program_id(0)

    @pl.when(step == 0)
    def _():
        for h in range(heads):
            beyond_ref[h] = entering_state(received, heads, size, h).astype(BF16)

    for h in range(heads):
        at = head_cols(h, size)
        beyond = beyond_ref[h]
        grad_key = grad_key_ref[:, at].astype(F32) + dot_nt(value_ref[:, at], beyond)
        grad_value = grad_value_ref[:, at].astype(F32) + dot_nn(key_ref[:, at], beyond)
        key_out_ref[:, at] = grad_key.astype(BF16)
        value_out_ref[:, at] = grad_value.astype(BF16)


def finish(keys, values, grad_key, grad_value, received, heads, size):
    rows, width = keys.shape
    step_rows = min(ROWS_AND_VMEM["finish"][0], rows)
    token = spec((step_rows, width), lambda i: (i, 0))
    return pl.pallas_call(
        functools.partial(finish_kernel, heads, size, len(received)),
        grid=(rows // step_rows,),
        in_specs=[token] * 4
        + [whole_spec(packed_shape(heads, size))] * len(received),
        out_specs=[token, token],
        out_shape=[jax.ShapeDtypeStruct((rows, width), BF16)] * 2,
        scratch_shapes=[pltpu.VMEM((heads, size, size), BF16)],
        compiler_params=params("finish"),
        cost_estimate=cost(4 * rows * width * size, 12 * rows * width),
        name="finish",
    )(keys, values, grad_key, grad_value, *received)


def send_on(value, count, hops, towards, senders):
    received = []
    for j in range(1, hops + 1):
        ahead = towards * j
        pairs = [(i, i + ahead) for i in range(count) if 0 <= i + ahead < count and (j == 1 or i in senders[j])]
        received.append(lax.ppermute(value, "seq", pairs) if pairs else jnp.zeros_like(value))
    return received


def exchange(value, count, hops, towards, parity, crowded, local):
    everyone = {j: range(count) for j in range(2, hops + 1)}
    some = {j: range(parity, count, 2) if j == 2 else () for j in range(2, hops + 1)}

    def branch(senders):
        def run(value):
            received = send_on(value, count, hops, towards, senders)
            return received, local()

        return run

    if hops == 1:
        return branch({})(value)
    return lax.switch(crowded, [branch(some), branch(everyone)], value)


def body(queries, keys, values, log_decay, gain, lengths, out_grad):
    rows, heads = log_decay.shape
    width = queries.shape[1]
    size = width // heads
    count = lax.axis_size("seq")
    groups = lax.axis_size("head")
    full_width = width * groups
    longest = rows * count // DOC_SHARE
    hops = max(1, min(count - 1, -(-(longest - 1) // rows)))
    first = (lax.axis_index("seq") * rows).astype(jnp.int32).reshape(1)
    gain = gain.reshape(1, width)

    state, factors, keep, *covered = local_states(
        keys, values, log_decay.T, lengths, first, count, heads, size
    )
    before, (raw, probs, states, query_in, key_out, value_out) = exchange(
        state, count, hops, 1, 0, covered[0][0],
        lambda: forward_local(queries, keys, values, factors, keep, heads, size),
    )
    raw, sums, entering = raw_and_sums(raw, query_in, out_grad, gain, before, heads, size)
    every = [sums] + [
        lax.ppermute(sums, "head", [(i, (i + j) % groups) for i in range(groups)]) for j in range(1, groups)
    ]
    carry, scale = carry_states(raw, query_in, out_grad, gain, state, every, full_width, heads, size)
    after, (normed, grad_query, grad_key, grad_value) = exchange(
        carry, count, hops, -1, 1, covered[1][0],
        lambda: backward_local(
            queries, keys, values, raw, out_grad, gain, scale, factors, keep, probs, states, entering, heads, size
        ),
    )
    grad_key, grad_value = finish(key_out, value_out, grad_key, grad_value, after, heads, size)
    return (normed, grad_query, grad_key, grad_value)


def solution(mesh):
    token = P("seq", "head")
    in_specs = (token, token, token, token, P("head"), P(), token)
    return jax.shard_map(body, mesh=mesh, in_specs=in_specs, out_specs=(token,) * 4, check_vma=False)
```
